32 devices in a mesh: segment: 2 (over y), blk: 16 (over z, x, core).
Axes of the slice: x: 2, y: 2, z: 4, core: 2. Of those that a mesh axis runs over, the one named last changes fastest.
Arguments:
- inputs: bfloat16 [2, 128, 128, 256], P(None, 'blk'), may hold values from -6 to 6
- first_right: bfloat16 [4, 128, 128, 128], P('segment', 'blk'), may hold values from -0.5 to 0.5
- first_left: bfloat16 [4, 128, 128, 128], P('segment', 'blk'), may hold values from -0.5 to 0.5
- second_right: bfloat16 [4, 128, 128, 128], P('segment', 'blk'), may hold values from -0.5 to 0.5
- second_left: bfloat16 [4, 128, 128, 128], P('segment', 'blk'), may hold values from -0.5 to 0.5
- cotangent: bfloat16 [2, 128, 128, 256], P(None, 'blk'), may hold values from -6 to 6
- sections: int32 [2], replicated, may hold values from 1 to 2, as said below
Outputs:
- grad_first_right: float32 [4, 128, 128, 128], P('segment', 'blk')
- grad_first_left: float32 [4, 128, 128, 128], P('segment', 'blk')
- grad_second_right: float32 [4, 128, 128, 128], P('segment', 'blk')
- grad_second_left: float32 [4, 128, 128, 128], P('segment', 'blk')
The draws below stay inside these ranges and needn't reach their ends.
Inputs may be any that keep to these rules, and one draw needn't show every extreme that they name: Segment s runs its first sections[s] layer slots; at least one segment runs all 2 and at least one runs a single one.
All inputs are finite; a program needn't handle non-finite values.
Results may differ from the reference program's by a relative error of at most 0.019.
Values may be sent and summed in bfloat16 or wider, within the bound.
No kernel may reach another device: no remote copies, remote signals or barrier semaphores. Data moves between devices by JAX's collectives and lax.ppermute only.
A program may use at most 64 MiB of HBM per device.

```python
import jax
import jax.numpy as jnp

NB = 128
BS = 128
SLOTS = 2
MICRO = 2
TOK = 256
LAYERS = 4
N_SEGMENT = 2


def draw_sections(key, part):
    key = jax.random.fold_in(key, 7)
    key_counts, key_order = jax.random.split(key)
    counts = jax.random.randint(key_counts, (N_SEGMENT,), 1, SLOTS + 1)
    order = jax.random.permutation(key_order, N_SEGMENT)
    counts = counts.at[order[0]].set(SLOTS)
    counts = counts.at[order[1]].set(1)
    return counts.astype(jnp.int32)


def block_levels(own_key, dims, cuts, smallest, largest):
    gain, own = 1.0, jax.random.fold_in(own_key, 6)
    for axis_at, blocks in cuts:
        steps = jnp.exp(jax.random.uniform(jax.random.fold_in(own, axis_at), (blocks,), jnp.float32, smallest / len(cuts), largest / len(cuts)))
        gain = gain * jnp.repeat(steps, dims[axis_at] // blocks).reshape([-1 if axis == axis_at else 1 for axis in range(len(dims))])
    return gain


def gaussian(rng, extent, width, reach, cuts=(), dtype=jnp.bfloat16):
    entries = jax.random.normal(rng, extent, jnp.float32) * width
    if len(cuts) > 0:
        entries = block_levels(rng, extent, cuts, -0.22, 0.18) * entries
    return jnp.clip(entries, min=-reach, max=reach).astype(dtype)


def setup_inputs(seed: int = 0) -> dict:
    key_of = jax.random.split(jax.random.key(seed), 8)
    inputs = gaussian(key_of[0], (MICRO, NB, BS, TOK), 1.0, 6.0, ((1, 16),))
    first_right = gaussian(key_of[1], (LAYERS, NB, BS, BS), BS ** -0.5, 0.5, ((0, 2), (1, 16)))
    first_left = gaussian(key_of[2], (LAYERS, NB, BS, BS), BS ** -0.5, 0.5, ((0, 2), (1, 16)))
    second_right = gaussian(key_of[3], (LAYERS, NB, BS, BS), BS ** -0.5, 0.5, ((0, 2), (1, 16)))
    second_left = gaussian(key_of[4], (LAYERS, NB, BS, BS), BS ** -0.5, 0.5, ((0, 2), (1, 16)))
    cotangent = gaussian(key_of[5], (MICRO, NB, BS, TOK), 1.0, 6.0, ((1, 16),))
    sections = draw_sections(jax.random.fold_in(key_of[7], 71), 0)
    return dict(inputs=inputs, first_right=first_right, first_left=first_left, second_right=second_right, second_left=second_left, cotangent=cotangent, sections=sections)


def factor(weight, values):
    return jnp.einsum('bij,bit->bjt', weight.astype(jnp.float32), values.astype(jnp.float32))

def permute_full(values):
    return jnp.swapaxes(values, 0, 1)

def monarch(right, left, values):
    mixed = factor(right, values).astype(jnp.bfloat16)
    permuted = permute_full(mixed)
    outer = factor(left, permuted).astype(jnp.bfloat16)
    return (permuted, permute_full(outer))

def monarch_back(right, left, values, permuted, grad_out):
    grad_c = permute_full(grad_out).astype(jnp.float32)
    grad_left = jnp.einsum('jbt,jkt->jbk', permuted.astype(jnp.float32), grad_c)
    grad_p = jnp.einsum('jbk,jkt->jbt', left.astype(jnp.float32), grad_c).astype(jnp.bfloat16)
    grad_a = permute_full(grad_p).astype(jnp.float32)
    grad_right = jnp.einsum('bit,bjt->bij', values.astype(jnp.float32), grad_a)
    grad_in = jnp.einsum('bij,bjt->bit', right.astype(jnp.float32), grad_a)
    return (grad_in, grad_right, grad_left)

def reference(inputs, first_right, first_left, second_right, second_left, cotangent, sections):
    shape_w = first_right.shape
    totals = [jnp.zeros(shape_w, jnp.float32) for index in range(4)]
    for micro in range(MICRO):
        state = inputs[micro]
        kept = []
        for layer in range(LAYERS):
            active = layer % SLOTS < sections[layer // SLOTS]
            p_one, upper = monarch(first_right[layer], first_left[layer], state)
            hidden = jax.nn.gelu(upper.astype(jnp.float32)).astype(jnp.bfloat16)
            p_two, branch = monarch(second_right[layer], second_left[layer], hidden)
            result = (state.astype(jnp.float32) + branch.astype(jnp.float32)).astype(jnp.bfloat16)
            kept.append((state, p_one, upper, hidden, p_two))
            state = jnp.where(active, result, state)
        grad = cotangent[micro]
        for layer in reversed(range(LAYERS)):
            active = layer % SLOTS < sections[layer // SLOTS]
            state_in, p_one, upper, hidden, p_two = kept[layer]
            grad_h, g_r2, g_l2 = monarch_back(second_right[layer], second_left[layer], hidden, p_two, grad)
            gelu_back = jax.vjp(jax.nn.gelu, upper.astype(jnp.float32))[1]
            grad_u = gelu_back(grad_h)[0].astype(jnp.bfloat16)
            grad_x, g_r1, g_l1 = monarch_back(first_right[layer], first_left[layer], state_in, p_one, grad_u)
            new_grad = (grad.astype(jnp.float32) + grad_x).astype(jnp.bfloat16)
            parts = (g_r1, g_l1, g_r2, g_l2)
            for index in range(4):
                totals[index] = totals[index].at[layer].add(jnp.where(active, parts[index], 0.0))
            grad = jnp.where(active, new_grad, grad)
    return (totals[0], totals[1], totals[2], totals[3])
```

```python
import functools
import math

import jax
import jax.numpy as jnp
from jax import lax
from jax.experimental import pallas as pl
from jax.experimental.pallas import tpu as pltpu
from jax.sharding import PartitionSpec as P

F32 = jnp.float32
BF16 = jnp.bfloat16
ROOT = math.sqrt(2.0 / math.pi)


def gelu(u):
    return 0.5 * u * (1.0 + jnp.tanh(ROOT * (u + 0.044715 * (u * u * u))))


def gelu_slope(u):
    square = u * u
    th = jnp.tanh(ROOT * (u + 0.044715 * (u * square)))
    inner = ROOT * (1.0 + 3 * 0.044715 * square)
    return 0.5 * (1.0 + th) + 0.5 * u * (1.0 - th * th) * inner


class Plan:
    def __init__(self, segments, devices, micros, blocks, tokens):
        self.segments = segments
        self.halves = 2 if micros * tokens >= 256 * segments and devices % 2 == 0 else 1
        self.group = devices // self.halves
        self.own = blocks // devices
        self.held = self.own * self.halves
        self.size = blocks
        self.tokens = micros * tokens // (segments * self.halves)
        self.kernels = segments == 2 and self.own % 8 == 0 and self.held % 16 == 0
        self.kernels = self.kernels and self.tokens % 128 == 0
        self.groups = None
        if self.halves > 1:
            self.groups = [
                [half * self.group + rank for rank in range(self.group)]
                for half in range(self.halves)
            ]

    def packed_shape(self):
        return (self.group, self.held, self.held, self.tokens)

    def natural_shape(self):
        return (self.held, self.size, self.tokens)

    def pack(self, values):
        split = values.reshape(self.held, self.halves, self.group, self.own, self.tokens)
        return split.transpose(2, 1, 3, 0, 4).reshape(self.packed_shape())

    def unpack(self, packed):
        split = packed.reshape(self.group, self.held, self.halves, self.own, self.tokens)
        return split.transpose(1, 2, 0, 3, 4).reshape(self.natural_shape())

    def exchange(self, packed):
        return lax.all_to_all(packed, "blk", 0, 0, axis_index_groups=self.groups, tiled=True)

    def swap_halves(self, value):
        devices = self.group * self.halves
        return lax.ppermute(
            value, "blk", [(at, (at + self.group) % devices) for at in range(devices)]
        )


def matmul(a, b, over_a, over_b):
    return lax.dot_general(a, b, (((over_a,), (over_b,)), ((), ())), preferred_element_type=F32)


def read_natural(plan, ref, block):
    values = ref[:, block].astype(F32)
    rows = [
        values[rank, half * plan.own : (half + 1) * plan.own]
        for half in range(plan.halves)
        for rank in range(plan.group)
    ]
    return jnp.concatenate(rows, axis=0)


def write_packed(plan, scratch, out):
    step = plan.group * plan.own * plan.held
    for half in range(plan.halves):
        rows = scratch[half * step : (half + 1) * step, :].astype(BF16)
        out[:, half * plan.own : (half + 1) * plan.own] = rows.reshape(
            plan.group, plan.own, plan.held, plan.tokens
        )


def scatter(plan, scratch, block, values):
    scratch[pl.ds(block, plan.size, stride=plan.held), :] = values


def call(plan, body, ins, outs, scratch, flops):
    shapes = [jax.ShapeDtypeStruct(shape, dtype) for shape, dtype in outs]
    volume = sum(math.prod(i.shape) * i.dtype.itemsize for i in ins)
    volume += sum(math.prod(s.shape) * s.dtype.itemsize for s in shapes)
    vmem = pl.BlockSpec(memory_space=pltpu.VMEM)
    return pl.pallas_call(
        functools.partial(body, plan),
        out_shape=shapes,
        in_specs=[vmem] * len(ins),
        out_specs=[vmem] * len(shapes),
        scratch_shapes=[pltpu.VMEM((plan.size * plan.held, plan.tokens), F32)] if scratch else [],
        compiler_params=pltpu.CompilerParams(vmem_limit_bytes=32 * 1024 * 1024),
        cost_estimate=pl.CostEstimate(flops=flops, bytes_accessed=volume, transcendentals=0),
    )(*ins)


def first_body(plan, state, weight, out, scratch):
    for block in range(plan.held):
        scatter(plan, scratch, block, matmul(weight[block], state[block], 0, 0))
    write_packed(plan, scratch, out)


def residual_body(plan, state, branch, weight, out, result, scratch):
    for block in range(plan.held):
        total = state[block].astype(F32) + read_natural(plan, branch, block)
        total = total.astype(BF16)
        result[block] = total
        scatter(plan, scratch, block, matmul(weight[block], total, 0, 0))
    write_packed(plan, scratch, out)


def left_body(plan, values, weight, out, kept, scratch):
    for block in range(plan.held):
        natural = read_natural(plan, values, block).astype(BF16)
        kept[block] = natural
        scatter(plan, scratch, block, matmul(weight[block], natural, 0, 0))
    write_packed(plan, scratch, out)


def gelu_body(plan, values, weight, out, upper, hidden, scratch):
    for block in range(plan.held):
        natural = read_natural(plan, values, block)
        upper[block] = natural.astype(BF16)
        active = gelu(natural).astype(BF16)
        hidden[block] = active
        scatter(plan, scratch, block, matmul(weight[block], active, 0, 0))
    write_packed(plan, scratch, out)


def pack_body(plan, values, out, scratch):
    for block in range(plan.held):
        scatter(plan, scratch, block, values[block].astype(F32))
    write_packed(plan, scratch, out)


def back_left_body(plan, grad, kept, weight, out, grad_weight, scratch):
    for block in range(plan.held):
        natural = read_natural(plan, grad, block).astype(BF16)
        scatter(plan, scratch, block, matmul(weight[block], natural, 1, 0))
        grad_weight[block] = matmul(kept[block], natural, 1, 1).astype(BF16)
    write_packed(plan, scratch, out)


def back_gelu_body(plan, grad, hidden, upper, weight, out, grad_weight, scratch):
    for block in range(plan.held):
        natural = read_natural(plan, grad, block).astype(BF16)
        grad_hidden = matmul(weight[block], natural, 1, 0)
        scatter(plan, scratch, block, grad_hidden * gelu_slope(upper[block].astype(F32)))
        grad_weight[block] = matmul(hidden[block], natural, 1, 1).astype(BF16)
    write_packed(plan, scratch, out)


def back_right_body(plan, grad, state, above, weight, out, result, grad_weight, scratch):
    for block in range(plan.held):
        natural = read_natural(plan, grad, block).astype(BF16)
        total = matmul(weight[block], natural, 1, 0) + above[block].astype(F32)
        result[block] = total.astype(BF16)
        scatter(plan, scratch, block, total)
        grad_weight[block] = matmul(state[block], natural, 1, 1).astype(BF16)
    write_packed(plan, scratch, out)


def outer_body(plan, grad, state, grad_weight):
    for block in range(plan.held):
        natural = read_natural(plan, grad, block).astype(BF16)
        grad_weight[block] = matmul(state[block], natural, 1, 1).astype(BF16)


def unpack_body(plan, values, out):
    for block in range(plan.held):
        out[block] = read_natural(plan, values, block).astype(BF16)


def apply(weight, values):
    return jnp.einsum("bij,bit->bjt", weight, values, preferred_element_type=F32)


def apply_back(weight, values):
    return jnp.einsum("bij,bjt->bit", weight, values, preferred_element_type=F32)


def outer(values, grad):
    return jnp.einsum("bit,bjt->bij", values, grad, preferred_element_type=F32).astype(BF16)


class Steps:
    def __init__(self, plan):
        self.plan = plan
        self.packed = (plan.packed_shape(), BF16)
        self.natural = (plan.natural_shape(), BF16)
        self.square = ((plan.held, plan.size, plan.size), BF16)
        self.flops = 2 * plan.held * plan.size * plan.size * plan.tokens

    def run(self, body, ins, outs, scratch=True, products=1):
        return call(self.plan, body, ins, outs, scratch, products * self.flops)

    def first(self, state, weight):
        if self.plan.kernels:
            return self.run(first_body, (state, weight), [self.packed])[0]
        return self.plan.pack(apply(weight, state).astype(BF16))

    def residual(self, state, branch, weight, active):
        if self.plan.kernels:
            return self.run(residual_body, (state, branch, weight), [self.packed, self.natural])
        total = (state.astype(F32) + self.plan.unpack(branch).astype(F32)).astype(BF16)
        total = jnp.where(active, total, state)
        return self.plan.pack(apply(weight, total).astype(BF16)), total

    def left(self, values, weight):
        if self.plan.kernels:
            return self.run(left_body, (values, weight), [self.packed, self.natural])
        natural = self.plan.unpack(values)
        return self.plan.pack(apply(weight, natural).astype(BF16)), natural

    def gelu(self, values, weight):
        if self.plan.kernels:
            outs = [self.packed, self.natural, self.natural]
            return self.run(gelu_body, (values, weight), outs)
        upper = self.plan.unpack(values)
        hidden = gelu(upper.astype(F32)).astype(BF16)
        return self.plan.pack(apply(weight, hidden).astype(BF16)), upper, hidden

    def pack(self, values):
        if self.plan.kernels:
            return self.run(pack_body, (values,), [self.packed], products=0)[0]
        return self.plan.pack(values)

    def unpack(self, values):
        if self.plan.kernels:
            return self.run(unpack_body, (values,), [self.natural], False, 0)[0]
        return self.plan.unpack(values)

    def back_left(self, grad, kept, weight):
        if self.plan.kernels:
            outs = [self.packed, self.square]
            return self.run(back_left_body, (grad, kept, weight), outs, products=2)
        natural = self.plan.unpack(grad)
        back = apply_back(weight, natural).astype(BF16)
        return self.plan.pack(back), outer(kept, natural)

    def back_gelu(self, grad, hidden, upper, weight):
        if self.plan.kernels:
            outs = [self.packed, self.square]
            return self.run(back_gelu_body, (grad, hidden, upper, weight), outs, products=2)
        natural = self.plan.unpack(grad)
        back = apply_back(weight, natural) * gelu_slope(upper.astype(F32))
        return self.plan.pack(back.astype(BF16)), outer(hidden, natural)

    def back_right(self, grad, state, above, weight, active):
        if self.plan.kernels:
            outs = [self.packed, self.natural, self.square]
            return self.run(back_right_body, (grad, state, above, weight), outs, products=2)
        natural = self.plan.unpack(grad)
        total = (apply_back(weight, natural) + above.astype(F32)).astype(BF16)
        total = jnp.where(active, total, above)
        return self.plan.pack(total), total, outer(state, natural)

    def outer(self, grad, state):
        if self.plan.kernels:
            return self.run(outer_body, (grad, state), [self.square], False)[0]
        return outer(state, self.plan.unpack(grad))


def spread(plan, factor, owner, half):
    mine = lax.axis_index("segment")
    if plan.segments == 2:
        other = lax.ppermute(factor, "segment", [(0, 1), (1, 0)])
        factor = jnp.where(owner == mine, factor, other)
    else:
        every = lax.all_gather(factor, "segment", axis=0)
        factor = lax.dynamic_index_in_dim(every, owner, 0, keepdims=False)
    if plan.halves == 1:
        return factor
    other = plan.swap_halves(factor)
    lower = jnp.where(half == 0, factor, other)
    upper = jnp.where(half == 0, other, factor)
    return jnp.concatenate([lower, upper], axis=1)


def collect(plan, parts, half):
    if plan.halves == 1:
        total = parts.astype(F32)
    else:
        lower, upper = parts[:, : plan.own], parts[:, plan.own :]
        kept = jnp.where(half == 0, lower, upper)
        other = plan.swap_halves(jnp.where(half == 0, upper, lower))
        total = kept.astype(F32) + other.astype(F32)
    if plan.segments == 2:
        other = lax.ppermute(total.astype(BF16), "segment", [(0, 1), (1, 0)])
        return total + other.astype(F32)
    return lax.psum(total, "segment")


def token_chunk(plan, values, half):
    mine = lax.axis_index("segment")
    per_micro = values.shape[-1] // plan.tokens

    def chunk(at):
        at = mine * plan.halves + at
        micro = lax.dynamic_index_in_dim(values, at // per_micro, 0, keepdims=False)
        start = (at % per_micro) * plan.tokens
        return lax.dynamic_slice_in_dim(micro, start, plan.tokens, 2)

    if plan.halves == 1:
        return chunk(0)
    kept, other = chunk(half), plan.swap_halves(chunk(1 - half))
    lower = jnp.where(half == 0, kept, other)
    upper = jnp.where(half == 0, other, kept)
    return jnp.concatenate([lower, upper], axis=0)


def shards(inputs, first_right, first_left, second_right, second_left, cotangent, sections):
    segments = lax.axis_size("segment")
    segment = lax.axis_index("segment")
    devices = lax.axis_size("blk")
    slots = first_right.shape[0]
    plan = Plan(segments, devices, inputs.shape[0], inputs.shape[2], inputs.shape[3])
    steps = Steps(plan)
    half = lax.axis_index("blk") // plan.group
    factors = (first_right, first_left, second_right, second_left)

    count = segments * slots - 1
    ends = jnp.cumsum(sections)
    layers = []
    for index in range(count):
        owner = jnp.minimum(jnp.sum((index >= ends).astype(jnp.int32)), segments - 1)
        slot = jnp.clip(index - (ends[owner] - sections[owner]), 0, slots - 1)
        layers.append((owner, slot, index < ends[-1]))

    weights = []
    for index, (owner, slot, active) in enumerate(layers):
        picked = [lax.dynamic_index_in_dim(f, slot, 0, keepdims=True) for f in factors]
        if index == 0:
            first = spread(plan, picked[0], owner, half)
            rest = spread(plan, jnp.concatenate(picked[1:], axis=0), owner, half)
            weights.append((first[0], rest[0], rest[1], rest[2]))
        else:
            every = spread(plan, jnp.concatenate(picked, axis=0), owner, half)
            weights.append((every[0], every[1], every[2], every[3]))

    state = token_chunk(plan, inputs, half)
    grad = token_chunk(plan, cotangent, half)

    saved = []
    branch = None
    for index in range(count):
        w = weights[index]
        if index == 0:
            sent = steps.first(state, w[0])
        else:
            sent, state = steps.residual(state, branch, w[0], layers[index - 1][2])
        sent, inner_one = steps.left(plan.exchange(sent), w[1])
        sent, upper, hidden = steps.gelu(plan.exchange(sent), w[2])
        if index < count - 1:
            sent, inner_two = steps.left(plan.exchange(sent), w[3])
            branch = plan.exchange(sent)
        else:
            inner_two = steps.unpack(plan.exchange(sent))
        saved.append((state, inner_one, upper, hidden, inner_two))

    totals = [None] * count
    sent = steps.pack(grad)
    for index in reversed(range(count)):
        w = weights[index]
        state, inner_one, upper, hidden, inner_two = saved[index]
        sent, grad_l2 = steps.back_left(plan.exchange(sent), inner_two, w[3])
        sent, grad_r2 = steps.back_gelu(plan.exchange(sent), hidden, upper, w[2])
        sent, grad_l1 = steps.back_left(plan.exchange(sent), inner_one, w[1])
        if index > 0:
            sent, grad, grad_r1 = steps.back_right(
                plan.exchange(sent), state, grad, w[0], layers[index][2]
            )
            every = collect(plan, jnp.stack([grad_r1, grad_l1, grad_r2, grad_l2]), half)
            totals[index] = (every[0], every[1], every[2], every[3])
        else:
            late = collect(plan, jnp.stack([grad_l1, grad_r2, grad_l2]), half)
            grad_r1 = steps.outer(plan.exchange(sent), state)
            last = collect(plan, grad_r1[None], half)
            totals[index] = (last[0], late[0], late[1], late[2])

    outs = []
    for at in range(4):
        rows = []
        for place in range(slots):
            total = jnp.zeros(first_right.shape[1:], F32)
            for index, (owner, slot, active) in enumerate(layers):
                here = active & (owner == segment) & (slot == place)
                total = jnp.where(here, totals[index][at], total)
            rows.append(total)
        outs.append(jnp.stack(rows))
    return tuple(outs)


def solution(mesh):
    whole = P("segment", "blk", None, None)
    tokens = P(None, "blk", None, None)
    in_specs = (tokens, whole, whole, whole, whole, tokens, P())
    return jax.shard_map(
        shards, mesh=mesh, in_specs=in_specs, out_specs=(whole,) * 4, check_vma=False
    )
```

```python
import functools
import math

import jax
import jax.numpy as jnp
from jax import lax
from jax.experimental import pallas as pl
from jax.experimental.pallas import tpu as pltpu
from jax.sharding import PartitionSpec as P

F32 = jnp.float32
BF16 = jnp.bfloat16
ROOT = math.sqrt(2.0 / math.pi)


def gelu(u):
    return 0.5 * u * (1.0 + jnp.tanh(ROOT * (u + 0.044715 * (u * u * u))))


def gelu_slope(u):
    square = u * u
    th = jnp.tanh(ROOT * (u + 0.044715 * (u * square)))
    inner = ROOT * (1.0 + 3 * 0.044715 * square)
    return 0.5 * (1.0 + th) + 0.5 * u * (1.0 - th * th) * inner


class Plan:
    def __init__(self, segments, devices, micros, blocks, tokens):
        self.segments = segments
        self.devices = devices
        self.halves = 2 if micros * tokens >= 256 * segments and devices % 2 == 0 else 1
        self.group = devices // self.halves
        self.own = blocks // devices
        self.held = self.own * self.halves
        self.size = blocks
        self.tokens = micros * tokens // (segments * self.halves)
        self.kernels = segments == 2 and micros == 2 and self.halves == 2
        self.kernels = self.kernels and self.own == 8 and self.tokens % 128 == 0
        self.groups = None
        if self.halves > 1:
            self.groups = [
                [half * self.group + rank for rank in range(self.group)]
                for half in range(self.halves)
            ]

    def packed_shape(self):
        return (self.group, self.held, self.held, self.tokens)

    def natural_shape(self):
        return (self.held, self.size, self.tokens)

    def pack(self, values):
        split = values.reshape(self.held, self.halves, self.group, self.own, self.tokens)
        return split.transpose(2, 1, 3, 0, 4).reshape(self.packed_shape())

    def unpack(self, packed):
        split = packed.reshape(self.group, self.held, self.halves, self.own, self.tokens)
        return split.transpose(1, 2, 0, 3, 4).reshape(self.natural_shape())

    def exchange(self, packed):
        return lax.all_to_all(packed, "blk", 0, 0, axis_index_groups=self.groups, tiled=True)

    def swap_halves(self, value):
        return lax.ppermute(
            value, "blk", [(at, (at + self.group) % self.devices) for at in range(self.devices)]
        )


def matmul(a, b, over_a, over_b):
    return lax.dot_general(a, b, (((over_a,), (over_b,)), ((), ())), preferred_element_type=F32)


def each_block(plan, half):
    for turn in range(2):
        base = (half[0] if turn == 0 else 1 - half[0]) * plan.own
        for at in range(plan.own):
            yield turn, at, turn * plan.own + at, base + at


def read_natural(plan, ref, block):
    values = ref[:, block].astype(F32)
    rows = [
        values[rank, half * plan.own : (half + 1) * plan.own]
        for half in range(plan.halves)
        for rank in range(plan.group)
    ]
    return jnp.concatenate(rows, axis=0)


def write_packed(plan, scratch, out):
    step = plan.group * plan.own * plan.held
    for half in range(plan.halves):
        rows = scratch[half * step : (half + 1) * step, :].astype(BF16)
        out[:, half * plan.own : (half + 1) * plan.own] = rows.reshape(
            plan.group, plan.own, plan.held, plan.tokens
        )


def scatter(plan, scratch, block, values):
    scratch[pl.ds(block, plan.size, stride=plan.held), :] = values


def start_body(plan, state, weight, out, scratch):
    for block in range(plan.own):
        values = matmul(weight[block], state[block], 0, 0)
        for part in range(plan.halves):
            chunk = values[:, part * plan.tokens : (part + 1) * plan.tokens]
            scratch[part, pl.ds(block, plan.size, stride=plan.own), :] = chunk
    step = plan.own * plan.own
    for part in range(plan.halves):
        for half in range(plan.halves):
            for rank in range(plan.group):
                at = (half * plan.group + rank) * step
                rows = scratch[part, at : at + step, :].astype(BF16)
                out[part * plan.group + rank, half * step : (half + 1) * step] = rows


def wide_left_body(plan, half, values, own, other, out, kept, scratch):
    for turn in range(2):
        base = (half[0] if turn == 0 else 1 - half[0]) * plan.own * plan.own
        weight = own if turn == 0 else other
        for pair in range(plan.own // 2):
            start = pl.multiple_of(base + pair * 2 * plan.own, 2 * plan.own)
            rows = values[:, pl.ds(start, 2 * plan.own), :].astype(F32)
            for odd in range(2):
                at = 2 * pair + odd
                natural = rows[:, odd * plan.own : (odd + 1) * plan.own]
                natural = natural.reshape(plan.size, plan.tokens).astype(BF16)
                kept[turn * plan.own + at] = natural
                block = (half[0] if turn == 0 else 1 - half[0]) * plan.own + at
                scatter(plan, scratch, block, matmul(weight[at], natural, 0, 0))
    write_packed(plan, scratch, out)


def residual_body(plan, half, state, branch, own, other, out, result, scratch):
    for turn, at, place, block in each_block(plan, half):
        total = state[place].astype(F32) + read_natural(plan, branch, block)
        total = total.astype(BF16)
        result[place] = total
        scatter(plan, scratch, block, matmul((own, other)[turn][at], total, 0, 0))
    write_packed(plan, scratch, out)


def left_body(plan, half, values, own, other, out, kept, scratch):
    for turn, at, place, block in each_block(plan, half):
        natural = read_natural(plan, values, block).astype(BF16)
        kept[place] = natural
        scatter(plan, scratch, block, matmul((own, other)[turn][at], natural, 0, 0))
    write_packed(plan, scratch, out)


def gelu_body(plan, half, values, own, other, out, upper, hidden, scratch):
    for turn, at, place, block in each_block(plan, half):
        natural = read_natural(plan, values, block)
        upper[place] = natural.astype(BF16)
        active = gelu(natural).astype(BF16)
        hidden[place] = active
        scatter(plan, scratch, block, matmul((own, other)[turn][at], active, 0, 0))
    write_packed(plan, scratch, out)


def pack_body(plan, half, values, out, scratch):
    for turn, at, place, block in each_block(plan, half):
        scatter(plan, scratch, block, values[place].astype(F32))
    write_packed(plan, scratch, out)


def unpack_body(plan, half, values, out):
    for turn, at, place, block in each_block(plan, half):
        out[place] = read_natural(plan, values, block).astype(BF16)


def put_grad(grads, turn, at, values):
    grads[turn][at] = values.astype(grads[turn].dtype)


def back_left_body(plan, half, grad, kept, own, other, out, stay, leave, scratch):
    for turn, at, place, block in each_block(plan, half):
        natural = read_natural(plan, grad, block).astype(BF16)
        scatter(plan, scratch, block, matmul((own, other)[turn][at], natural, 1, 0))
        put_grad((stay, leave), turn, at, matmul(kept[place], natural, 1, 1))
    write_packed(plan, scratch, out)


def last_left_body(plan, half, grad, kept, own, other, out, stay, leave, scratch):
    for turn, at, place, block in each_block(plan, half):
        natural = read_natural(plan, grad, block).astype(BF16)
        scatter(plan, scratch, block, matmul((own, other)[turn][at], natural, 1, 0))
        put_grad((stay, leave), turn, at, matmul(kept[place], natural, 1, 1))
    out[...] = scratch[...].astype(BF16).reshape(plan.devices, plan.size, plan.tokens)


def back_gelu_body(plan, half, grad, hidden, upper, own, other, out, stay, leave, scratch):
    for turn, at, place, block in each_block(plan, half):
        natural = read_natural(plan, grad, block).astype(BF16)
        grad_hidden = matmul((own, other)[turn][at], natural, 1, 0)
        scatter(plan, scratch, block, grad_hidden * gelu_slope(upper[place].astype(F32)))
        put_grad((stay, leave), turn, at, matmul(hidden[place], natural, 1, 1))
    write_packed(plan, scratch, out)


def back_right_body(
    plan, half, grad, state, above, own, other, out, result, stay, leave, scratch
):
    for turn, at, place, block in each_block(plan, half):
        natural = read_natural(plan, grad, block).astype(BF16)
        total = matmul((own, other)[turn][at], natural, 1, 0) + above[place].astype(F32)
        result[place] = total.astype(BF16)
        scatter(plan, scratch, block, total)
        put_grad((stay, leave), turn, at, matmul(state[place], natural, 1, 1))
    write_packed(plan, scratch, out)


def end_body(plan, grad, state, stay, leave):
    for block in range(plan.own):
        total = jnp.zeros((plan.size, plan.size), F32)
        for part in range(plan.halves):
            rows = slice(block * plan.held, (block + 1) * plan.held)
            sources = slice(part * plan.group, (part + 1) * plan.group)
            values = grad[sources, rows].astype(F32)
            natural = jnp.concatenate(
                [
                    values[rank, half * plan.own : (half + 1) * plan.own]
                    for half in range(plan.halves)
                    for rank in range(plan.group)
                ],
                axis=0,
            ).astype(BF16)
            tokens = slice(part * plan.tokens, (part + 1) * plan.tokens)
            total = total + matmul(state[block, :, tokens], natural, 1, 1)
        stay[block] = total
        leave[block] = total.astype(BF16)


class Kernels:
    def __init__(self, plan, half):
        self.plan = plan
        self.half = half
        self.packed = (plan.packed_shape(), BF16)
        self.wide = ((plan.devices, plan.size, plan.tokens), BF16)
        self.natural = (plan.natural_shape(), BF16)
        square = (plan.own, plan.size, plan.size)
        self.grads = [(square, F32), (square, BF16)]
        self.rows = (plan.size * plan.held, plan.tokens)

    def run(self, body, ins, outs, scratch=None, products=1, after=(), half=True):
        plan = self.plan
        shapes = [jax.ShapeDtypeStruct(shape, dtype) for shape, dtype in outs]
        volume = sum(math.prod(i.shape) * i.dtype.itemsize for i in ins)
        volume += sum(math.prod(s.shape) * s.dtype.itemsize for s in shapes)
        flops = products * 2 * plan.held * plan.size * plan.size * plan.tokens
        vmem = pl.BlockSpec(memory_space=pltpu.VMEM)
        specs = [vmem] * len(ins)
        if half:
            ins = (self.half,) + tuple(ins)
            specs = [pl.BlockSpec(memory_space=pltpu.SMEM)] + specs
        first, count = len(ins), len(after)

        def kernel(*refs):
            body(plan, *refs[:first], *refs[first + count :])

        return pl.pallas_call(
            kernel,
            out_shape=shapes,
            in_specs=specs + [pl.BlockSpec(memory_space=pl.ANY)] * count,
            out_specs=[vmem] * len(shapes),
            scratch_shapes=[pltpu.VMEM(scratch, F32)] if scratch else [],
            compiler_params=pltpu.CompilerParams(vmem_limit_bytes=32 * 1024 * 1024),
            cost_estimate=pl.CostEstimate(flops=flops, bytes_accessed=volume, transcendentals=0),
            name=body.__name__,
        )(*ins, *after)


def swap_segments(value):
    return lax.ppermute(value, "segment", [(0, 1), (1, 0)])


def two_segments(plan, inputs, factors, cotangent, sections):
    segment = lax.axis_index("segment")
    half = lax.axis_index("blk") // plan.group
    kernels = Kernels(plan, half.astype(jnp.int32).reshape(1))
    run, packed, natural, grads = kernels.run, kernels.packed, kernels.natural, kernels.grads
    rows = kernels.rows
    count = 3

    owners = [jnp.int32(0), 2 - sections[0], jnp.int32(1)]
    places = [jnp.int32(0), sections[0] - 1, sections[1] - 1]

    def pick(index, factor, received):
        slot = places[index]
        mine = factor[0] if index == 0 else jnp.where(slot == 0, factor[0], factor[1])
        theirs = received[0] if index == 0 else jnp.where(slot == 0, received[0], received[1])
        return jnp.where(owners[index] == segment, mine, theirs)

    micro = lax.dynamic_index_in_dim(inputs, segment, 0, keepdims=False)
    above = lax.dynamic_index_in_dim(cotangent, segment, 0, keepdims=False)

    def own_and_other(values):
        lower, upper = values[:, :, : plan.tokens], values[:, :, plan.tokens :]
        kept = jnp.where(half == 0, lower, upper)
        leave = jnp.where(half == 0, upper, lower)
        return jnp.concatenate([kept, plan.swap_halves(leave)], axis=0)

    first = lax.ppermute(factors[0][0], "segment", [(0, 1)])
    first = jnp.where(segment == 0, factors[0][0], first)
    received = [None] * 4
    for at in (1, 2, 3, 0):
        received[at] = swap_segments(factors[at])
    weights = []
    for index in range(count):
        layer = []
        for at in range(4):
            if index == 0 and at == 0:
                layer.append((first, None))
                continue
            own = pick(index, factors[at], received[at])
            layer.append((own, plan.swap_halves(own)))
        weights.append(layer)

    sent = run(
        start_body,
        (micro, first),
        [kernels.wide],
        (plan.halves, plan.size * plan.own, plan.tokens),
        half=False,
    )[0]
    sent = lax.all_to_all(sent, "blk", 0, 0, tiled=True)
    state = own_and_other(micro)
    grad = own_and_other(above)

    saved = []
    branch = None
    for index in range(count):
        w = weights[index]
        if index == 0:
            body, values = wide_left_body, sent
        else:
            ins = (state, branch) + w[0]
            sent, state = run(residual_body, ins, [packed, natural], rows)
            body, values = left_body, plan.exchange(sent)
        sent, inner_one = run(body, (values,) + w[1], [packed, natural], rows)
        ins = (plan.exchange(sent),) + w[2]
        sent, upper, hidden = run(gelu_body, ins, [packed, natural, natural], rows)
        values = plan.exchange(sent)
        if index < count - 1:
            sent, inner_two = run(left_body, (values,) + w[3], [packed, natural], rows)
            branch = plan.exchange(sent)
        else:
            inner_two = run(unpack_body, (values,), [natural], products=0)[0]
        saved.append((state, inner_one, upper, hidden, inner_two))

    waiting = [(), ()]
    totals = [[None] * 4 for index in range(count)]

    def step(body, ins, outs, products=2):
        results = run(body, ins, outs + grads, rows, products, after=waiting.pop(0))
        stay, leave = results[-2:]
        other = plan.swap_halves(leave)
        waiting.append((other,))
        return results[:-2], stay.astype(F32) + other.astype(F32)

    def collect(index, values):
        if index == 0:
            other = [lax.ppermute(v.astype(BF16), "segment", [(1, 0)]) for v in values]
        else:
            other = swap_segments(jnp.stack([v.astype(BF16) for v in values]))
        return [value + other[at].astype(F32) for at, value in enumerate(values)]

    sent = run(pack_body, (grad,), [packed], rows, products=0)[0]
    for index in reversed(range(count)):
        w = weights[index]
        state, inner_one, upper, hidden, inner_two = saved[index]
        ins = (plan.exchange(sent), inner_two) + w[3]
        (sent,), grad_l2 = step(back_left_body, ins, [packed])
        ins = (plan.exchange(sent), hidden, upper) + w[2]
        (sent,), grad_r2 = step(back_gelu_body, ins, [packed])
        ins = (plan.exchange(sent), inner_one) + w[1]
        if index > 0:
            (sent,), grad_l1 = step(back_left_body, ins, [packed])
            ins = (plan.exchange(sent), state, grad) + w[0]
            (sent, grad), grad_r1 = step(back_right_body, ins, [packed, natural])
            totals[index] = collect(index, [grad_r1, grad_l1, grad_r2, grad_l2])
        else:
            (sent,), grad_l1 = step(last_left_body, ins, [kernels.wide])
            sent = lax.all_to_all(sent, "blk", 0, 0, tiled=True)
            stay, leave = run(end_body, (sent, micro), grads, half=False)
            other = lax.ppermute(leave, "segment", [(1, 0)])
            late = collect(index, [grad_l1, grad_r2, grad_l2])
            totals[index] = [stay + other.astype(F32)] + late

    outs = []
    for at in range(4):
        slots = []
        for place in range(2):
            total = jnp.zeros(factors[0].shape[1:], F32)
            for index in range(count):
                here = (owners[index] == segment) & (places[index] == place)
                total = jnp.where(here, totals[index][at], total)
            slots.append(total)
        outs.append(jnp.stack(slots))
    return tuple(outs)


def apply(weight, values):
    return jnp.einsum("bij,bit->bjt", weight, values, preferred_element_type=F32)


def apply_back(weight, values):
    return jnp.einsum("bij,bjt->bit", weight, values, preferred_element_type=F32)


def outer(values, grad):
    return jnp.einsum("bit,bjt->bij", values, grad, preferred_element_type=F32).astype(BF16)


def spread(plan, factor, owner, half):
    every = lax.all_gather(factor, "segment", axis=0)
    factor = lax.dynamic_index_in_dim(every, owner, 0, keepdims=False)
    if plan.halves == 1:
        return factor
    other = plan.swap_halves(factor)
    lower = jnp.where(half == 0, factor, other)
    upper = jnp.where(half == 0, other, factor)
    return jnp.concatenate([lower, upper], axis=1)


def collect(plan, parts, half):
    if plan.halves == 1:
        return lax.psum(parts.astype(F32), "segment")
    lower, upper = parts[:, : plan.own], parts[:, plan.own :]
    kept = jnp.where(half == 0, lower, upper)
    other = plan.swap_halves(jnp.where(half == 0, upper, lower))
    return lax.psum(kept.astype(F32) + other.astype(F32), "segment")


def token_chunk(plan, values, half):
    mine = lax.axis_index("segment")
    per_micro = values.shape[-1] // plan.tokens

    def chunk(at):
        at = mine * plan.halves + at
        micro = lax.dynamic_index_in_dim(values, at // per_micro, 0, keepdims=False)
        start = (at % per_micro) * plan.tokens
        return lax.dynamic_slice_in_dim(micro, start, plan.tokens, 2)

    if plan.halves == 1:
        return chunk(0)
    kept, other = chunk(half), plan.swap_halves(chunk(1 - half))
    lower = jnp.where(half == 0, kept, other)
    upper = jnp.where(half == 0, other, kept)
    return jnp.concatenate([lower, upper], axis=0)


def many_segments(plan, inputs, factors, cotangent, sections):
    segment = lax.axis_index("segment")
    half = lax.axis_index("blk") // plan.group
    slots = factors[0].shape[0]

    def trade(values):
        return plan.unpack(plan.exchange(plan.pack(values.astype(BF16))))

    count = plan.segments * slots - 1
    ends = jnp.cumsum(sections)
    layers, weights = [], []
    for index in range(count):
        owner = jnp.minimum(jnp.sum((index >= ends).astype(jnp.int32)), plan.segments - 1)
        slot = jnp.clip(index - (ends[owner] - sections[owner]), 0, slots - 1)
        layers.append((owner, slot, index < ends[-1]))
        picked = [lax.dynamic_index_in_dim(f, slot, 0, keepdims=True) for f in factors]
        weights.append(spread(plan, jnp.concatenate(picked, axis=0), owner, half))

    state = token_chunk(plan, inputs, half)
    grad = token_chunk(plan, cotangent, half)
    saved = []
    for index in range(count):
        w = weights[index]
        inner_one = trade(apply(w[0], state))
        upper = trade(apply(w[1], inner_one))
        hidden = gelu(upper.astype(F32)).astype(BF16)
        inner_two = trade(apply(w[2], hidden))
        saved.append((state, inner_one, upper, hidden, inner_two))
        if index < count - 1:
            branch = trade(apply(w[3], inner_two))
            total = (state.astype(F32) + branch.astype(F32)).astype(BF16)
            state = jnp.where(layers[index][2], total, state)

    totals = [None] * count
    for index in reversed(range(count)):
        w = weights[index]
        state, inner_one, upper, hidden, inner_two = saved[index]
        grad_c = trade(grad)
        grad_a = trade(apply_back(w[3], grad_c))
        parts = [outer(hidden, grad_a), outer(inner_two, grad_c)]
        grad_u = apply_back(w[2], grad_a) * gelu_slope(upper.astype(F32))
        grad_c = trade(grad_u)
        grad_a = trade(apply_back(w[1], grad_c))
        parts = [outer(state, grad_a), outer(inner_one, grad_c)] + parts
        totals[index] = collect(plan, jnp.stack(parts), half)
        total = (apply_back(w[0], grad_a) + grad.astype(F32)).astype(BF16)
        grad = jnp.where(layers[index][2], total, grad)

    outs = []
    for at in range(4):
        rows = []
        for place in range(slots):
            total = jnp.zeros(factors[0].shape[1:], F32)
            for index, (owner, slot, active) in enumerate(layers):
                here = active & (owner == segment) & (slot == place)
                total = jnp.where(here, totals[index][at], total)
            rows.append(total)
        outs.append(jnp.stack(rows))
    return tuple(outs)


def shards(inputs, first_right, first_left, second_right, second_left, cotangent, sections):
    segments = lax.axis_size("segment")
    devices = lax.axis_size("blk")
    plan = Plan(segments, devices, inputs.shape[0], inputs.shape[2], inputs.shape[3])
    factors = (first_right, first_left, second_right, second_left)
    run = two_segments if plan.kernels else many_segments
    return run(plan, inputs, factors, cotangent, sections)


def solution(mesh):
    whole = P("segment", "blk", None, None)
    tokens = P(None, "blk", None, None)
    in_specs = (tokens, whole, whole, whole, whole, tokens, P())
    return jax.shard_map(
        shards, mesh=mesh, in_specs=in_specs, out_specs=(whole,) * 4, check_vma=False
    )
```

```python
import functools
import math

import jax
import jax.numpy as jnp
from jax import lax
from jax.experimental import pallas as pl
from jax.experimental.pallas import tpu as pltpu
from jax.sharding import PartitionSpec as P

F32 = jnp.float32
BF16 = jnp.bfloat16
ROOT = math.sqrt(2.0 / math.pi)


def gelu(u):
    return 0.5 * u * (1.0 + jnp.tanh(ROOT * (u + 0.044715 * (u * u * u))))


def gelu_slope(u):
    square = u * u
    th = jnp.tanh(ROOT * (u + 0.044715 * (u * square)))
    inner = ROOT * (1.0 + 3 * 0.044715 * square)
    return 0.5 * (1.0 + th) + 0.5 * u * (1.0 - th * th) * inner


class Plan:
    def __init__(self, segments, devices, micros, blocks, tokens):
        self.segments = segments
        self.devices = devices
        self.halves = 2 if micros * tokens >= 256 * segments and devices % 2 == 0 else 1
        self.group = devices // self.halves
        self.own = blocks // devices
        self.held = self.own * self.halves
        self.size = blocks
        self.tokens = micros * tokens // (segments * self.halves)
        self.kernels = segments == 2 and micros == 2 and self.own == 8 and tokens % 128 == 0
        self.groups = None
        if self.halves > 1:
            self.groups = [
                [half * self.group + rank for rank in range(self.group)]
                for half in range(self.halves)
            ]

    def packed_shape(self):
        return (self.group, self.held, self.held, self.tokens)

    def natural_shape(self):
        return (self.held, self.size, self.tokens)

    def pack(self, values):
        split = values.reshape(self.held, self.halves, self.group, self.own, self.tokens)
        return split.transpose(2, 1, 3, 0, 4).reshape(self.packed_shape())

    def unpack(self, packed):
        split = packed.reshape(self.group, self.held, self.halves, self.own, self.tokens)
        return split.transpose(1, 2, 0, 3, 4).reshape(self.natural_shape())

    def exchange(self, packed):
        return lax.all_to_all(packed, "blk", 0, 0, axis_index_groups=self.groups, tiled=True)

    def swap_halves(self, value):
        return lax.ppermute(
            value, "blk", [(at, (at + self.group) % self.devices) for at in range(self.devices)]
        )


def matmul(a, b, over_a, over_b):
    return lax.dot_general(a, b, (((over_a,), (over_b,)), ((), ())), preferred_element_type=F32)


def read(plan, ref, at):
    pair = slice(at // 2 * 2 * plan.own, (at // 2 + 1) * 2 * plan.own)
    rows = ref[:, pair].astype(F32)[:, at % 2 * plan.own : (at % 2 + 1) * plan.own]
    return rows.reshape(plan.size, rows.shape[-1])


def start_work(plan, at, scatter, weight, gradient, state):
    scatter(matmul(weight, state[at], 0, 0))


def residual_work(plan, at, scatter, weight, gradient, branch, state, result):
    total = (state[at].astype(F32) + read(plan, branch, at)).astype(BF16)
    result[at] = total
    scatter(matmul(weight, total, 0, 0))


def left_work(plan, at, scatter, weight, gradient, values, kept):
    natural = read(plan, values, at).astype(BF16)
    kept[at] = natural
    scatter(matmul(weight, natural, 0, 0))


def gelu_work(plan, at, scatter, weight, gradient, values, upper, hidden):
    natural = read(plan, values, at)
    upper[at] = natural.astype(BF16)
    active = gelu(natural).astype(BF16)
    hidden[at] = active
    scatter(matmul(weight, active, 0, 0))


def pack_work(plan, at, scatter, weight, gradient, values):
    scatter(values[at].astype(F32))


def unpack_work(plan, at, scatter, weight, gradient, values, out):
    out[at] = read(plan, values, at).astype(BF16)


def back_left_work(plan, at, scatter, weight, gradient, grad, kept):
    natural = read(plan, grad, at).astype(BF16)
    scatter(matmul(weight, natural, 1, 0))
    gradient(matmul(kept[at], natural, 1, 1))


def back_gelu_work(plan, at, scatter, weight, gradient, grad, hidden, upper):
    natural = read(plan, grad, at).astype(BF16)
    grad_hidden = matmul(weight, natural, 1, 0)
    scatter(grad_hidden * gelu_slope(upper[at].astype(F32)))
    gradient(matmul(hidden[at], natural, 1, 1))


def back_right_work(plan, at, scatter, weight, gradient, grad, state, above, result):
    natural = read(plan, grad, at).astype(BF16)
    total = matmul(weight, natural, 1, 0) + above[at].astype(F32)
    result[at] = total.astype(BF16)
    scatter(total)
    gradient(matmul(state[at], natural, 1, 1))


def end_work(plan, at, scatter, weight, gradient, grad, state):
    natural = read(plan, grad, at).astype(BF16)
    gradient(matmul(state[at], natural, 1, 1))


class Kernels:
    def __init__(self, plan, tokens, picks):
        self.plan = plan
        self.picks = picks
        self.tokens = tokens
        self.natural = (plan.own, plan.size, tokens)
        self.sent = (plan.devices, plan.own * plan.own, tokens)
        self.square = (plan.own, plan.size, plan.size)

    def run(self, work, ins, packed=0, weight=None, send=True, naturals=0, grads=False, after=()):
        plan, tokens, picks = self.plan, self.tokens, self.picks
        turn_blocks = plan.own // 2
        natural = pl.BlockSpec((turn_blocks,) + self.natural[1:], lambda turn, picks: (turn, 0, 0))
        arrived = pl.BlockSpec(
            (plan.devices, turn_blocks * plan.own, tokens), lambda turn, picks: (0, turn, 0)
        )
        square = (turn_blocks,) + self.square[1:]
        in_specs = [arrived] * packed + [natural] * (len(ins) - packed)
        operands = list(ins)
        layer, mine, theirs = weight or (0, None, None)
        matrices = [m for m in (mine, theirs) if m is not None]
        for matrix in matrices:
            operands.append(matrix)
            if len(matrix.shape) == 4:
                spec = pl.BlockSpec(
                    (None,) + square, lambda turn, picks: (picks[2 * layer], turn, 0, 0)
                )
            else:
                spec = pl.BlockSpec(square, lambda turn, picks: (turn, 0, 0))
            in_specs.append(spec)
        operands += after
        in_specs += [pl.BlockSpec(memory_space=pl.ANY)] * len(after)
        outs, out_specs, scratch = [], [], []
        if send:
            outs.append(jax.ShapeDtypeStruct(self.sent, BF16))
            out_specs.append(pl.BlockSpec(self.sent, lambda turn, picks: (0, 0, 0)))
            scratch.append(pltpu.VMEM((tokens // 128, plan.size * plan.own, 128), F32))
        outs += [jax.ShapeDtypeStruct(self.natural, BF16)] * naturals
        out_specs += [natural] * naturals
        if grads:
            outs += [jax.ShapeDtypeStruct(self.square, dtype) for dtype in (F32, BF16)]
            out_specs += [pl.BlockSpec(square, lambda turn, picks: (turn, 0, 0))] * 2

        def kernel(picks, *refs):
            refs = list(refs)
            turn = pl.program_id(0)
            inner = [refs.pop(0) for i in ins]
            factors = [refs.pop(0) for i in matrices]
            del refs[: len(after)]
            out = refs.pop(0) if send else None
            inner += [refs.pop(0) for i in range(naturals)]
            gradients = [refs.pop(0) for i in range(2 if grads else 0)]
            store = refs[0] if send else None

            def scatter(at, values):
                rows = pl.ds(turn * turn_blocks + at, plan.size, stride=plan.own)
                for part in range(tokens // 128):
                    store[part, rows, :] = values[:, part * 128 : (part + 1) * 128]

            def gradient(at, values):
                for ref in gradients:
                    ref[at] = values.astype(ref.dtype)

            here = picks[2 * layer + 1] == 1
            for at in range(turn_blocks):
                matrix = None
                if len(factors) == 2:
                    matrix = jnp.where(here, factors[0][at], factors[1][at])
                elif factors:
                    matrix = factors[0][at]
                put = functools.partial(scatter, at)
                work(plan, at, put, matrix, functools.partial(gradient, at), *inner)
            if send:

                @pl.when(turn == 1)
                def _():
                    for part in range(tokens // 128):
                        rows = store[part].astype(BF16)
                        rows = rows.reshape(plan.devices, plan.own * plan.own, 128)
                        out[:, :, part * 128 : (part + 1) * 128] = rows

        volume = sum(math.prod(i.shape) * i.dtype.itemsize for i in ins)
        volume += sum(math.prod(o.shape) * o.dtype.itemsize for o in outs)
        products = (1 if matrices else 0) + (1 if grads else 0)
        flops = products * 2 * plan.own * plan.size * plan.size * tokens
        return pl.pallas_call(
            kernel,
            out_shape=outs,
            grid_spec=pltpu.PrefetchScalarGridSpec(
                num_scalar_prefetch=1,
                grid=(2,),
                in_specs=in_specs,
                out_specs=out_specs,
                scratch_shapes=scratch,
            ),
            compiler_params=pltpu.CompilerParams(
                vmem_limit_bytes=60 * 1024 * 1024, dimension_semantics=("arbitrary",)
            ),
            cost_estimate=pl.CostEstimate(flops=flops, bytes_accessed=volume, transcendentals=0),
            name=work.__name__,
        )(picks, *operands)


def two_segments(plan, inputs, factors, cotangent, sections):
    segment = lax.axis_index("segment")
    both = [(0, 1), (1, 0)]
    count = 3

    owners = [jnp.int32(0), 2 - sections[0], jnp.int32(1)]
    slots = [jnp.int32(0), sections[0] - 1, sections[1] - 1]
    picks = []
    for owner, slot in zip(owners, slots):
        picks += [jnp.clip(slot, 0, 1), (owner == segment).astype(jnp.int32)]
    kernels = Kernels(plan, inputs.shape[3], jnp.stack(picks).astype(jnp.int32))
    run = kernels.run

    def exchange(value):
        return lax.all_to_all(value, "blk", 0, 0, tiled=True)

    micro = lax.dynamic_index_in_dim(inputs, segment, 0, keepdims=False)
    grad = lax.dynamic_index_in_dim(cotangent, segment, 0, keepdims=False)
    early = lax.ppermute(factors[0][0], "segment", [(0, 1)])
    early = jnp.where(segment == 0, factors[0][0], early)
    received = [lax.ppermute(factor, "segment", both) for factor in factors]

    def weight(layer, at):
        if layer == 0 and at == 0:
            return layer, early, None
        return layer, factors[at], received[at]

    saved = []
    state, branch = micro, None
    for layer in range(count):
        if layer == 0:
            sent = run(start_work, (state,), 0, weight(0, 0))[0]
        else:
            sent, state = run(residual_work, (branch, state), 1, weight(layer, 0), naturals=1)
        sent, inner = run(left_work, (exchange(sent),), 1, weight(layer, 1), naturals=1)
        sent, upper, hidden = run(gelu_work, (exchange(sent),), 1, weight(layer, 2), naturals=2)
        values = exchange(sent)
        if layer < count - 1:
            sent, inner_two = run(left_work, (values,), 1, weight(layer, 3), naturals=1)
            branch = exchange(sent)
        else:
            inner_two = run(unpack_work, (values,), 1, send=False, naturals=1)[0]
        saved.append((state, inner, upper, hidden, inner_two))

    waiting = [(), ()]
    parts = [[None] * 4 for layer in range(count)]

    def step(layer, at, work, ins, naturals=0):
        after = waiting.pop(0)
        use = weight(layer, at)
        *results, stay, leave = run(work, ins, 1, use, True, naturals, True, after)
        other = lax.ppermute(leave, "segment", [(1, 0)] if layer == 0 else both)
        waiting.append((other,))
        parts[layer][at] = (stay, other)
        return results if naturals else results[0]

    sent = run(pack_work, (grad,))[0]
    for layer in reversed(range(count)):
        state, inner, upper, hidden, inner_two = saved[layer]
        sent = step(layer, 3, back_left_work, (exchange(sent), inner_two))
        sent = step(layer, 2, back_gelu_work, (exchange(sent), hidden, upper))
        sent = step(layer, 1, back_left_work, (exchange(sent), inner))
        if layer > 0:
            ins = (exchange(sent), state, grad)
            sent, grad = step(layer, 0, back_right_work, ins, 1)
    ins = (exchange(sent), state)
    stay, leave = run(end_work, ins, 1, send=False, grads=True, after=waiting.pop(0))
    parts[0][0] = (stay, lax.ppermute(leave, "segment", [(1, 0)]))

    outs = []
    first_has_two = sections[0] == 2
    for at in range(4):
        zero, one, two = [stay + other.astype(F32) for stay, other in (p[at] for p in parts)]
        low = jnp.where(segment == 0, zero, jnp.where(first_has_two, two, one))
        high = jnp.where(segment == 0, one, two)
        high = jnp.where(first_has_two == (segment == 0), high, 0.0)
        outs.append(jnp.stack([low, high]))
    return tuple(outs)


def apply(weight, values):
    return jnp.einsum("bij,bit->bjt", weight, values, preferred_element_type=F32)


def apply_back(weight, values):
    return jnp.einsum("bij,bjt->bit", weight, values, preferred_element_type=F32)


def outer(values, grad):
    return jnp.einsum("bit,bjt->bij", values, grad, preferred_element_type=F32).astype(BF16)


def spread(plan, factor, owner, half):
    every = lax.all_gather(factor, "segment", axis=0)
    factor = lax.dynamic_index_in_dim(every, owner, 0, keepdims=False)
    if plan.halves == 1:
        return factor
    other = plan.swap_halves(factor)
    lower = jnp.where(half == 0, factor, other)
    upper = jnp.where(half == 0, other, factor)
    return jnp.concatenate([lower, upper], axis=1)


def collect(plan, parts, half):
    if plan.halves == 1:
        return lax.psum(parts.astype(F32), "segment")
    lower, upper = parts[:, : plan.own], parts[:, plan.own :]
    kept = jnp.where(half == 0, lower, upper)
    other = plan.swap_halves(jnp.where(half == 0, upper, lower))
    return lax.psum(kept.astype(F32) + other.astype(F32), "segment")


def token_chunk(plan, values, half):
    mine = lax.axis_index("segment")
    per_micro = values.shape[-1] // plan.tokens

    def chunk(at):
        at = mine * plan.halves + at
        micro = lax.dynamic_index_in_dim(values, at // per_micro, 0, keepdims=False)
        start = (at % per_micro) * plan.tokens
        return lax.dynamic_slice_in_dim(micro, start, plan.tokens, 2)

    if plan.halves == 1:
        return chunk(0)
    kept, other = chunk(half), plan.swap_halves(chunk(1 - half))
    lower = jnp.where(half == 0, kept, other)
    upper = jnp.where(half == 0, other, kept)
    return jnp.concatenate([lower, upper], axis=0)


def many_segments(plan, inputs, factors, cotangent, sections):
    segment = lax.axis_index("segment")
    half = lax.axis_index("blk") // plan.group
    slots = factors[0].shape[0]

    def trade(values):
        return plan.unpack(plan.exchange(plan.pack(values.astype(BF16))))

    count = plan.segments * slots - 1
    ends = jnp.cumsum(sections)
    layers, weights = [], []
    for index in range(count):
        owner = jnp.minimum(jnp.sum((index >= ends).astype(jnp.int32)), plan.segments - 1)
        slot = jnp.clip(index - (ends[owner] - sections[owner]), 0, slots - 1)
        layers.append((owner, slot, index < ends[-1]))
        picked = [lax.dynamic_index_in_dim(f, slot, 0, keepdims=True) for f in factors]
        weights.append(spread(plan, jnp.concatenate(picked, axis=0), owner, half))

    state = token_chunk(plan, inputs, half)
    grad = token_chunk(plan, cotangent, half)
    saved = []
    for index in range(count):
        w = weights[index]
        inner_one = trade(apply(w[0], state))
        upper = trade(apply(w[1], inner_one))
        hidden = gelu(upper.astype(F32)).astype(BF16)
        inner_two = trade(apply(w[2], hidden))
        saved.append((state, inner_one, upper, hidden, inner_two))
        if index < count - 1:
            branch = trade(apply(w[3], inner_two))
            total = (state.astype(F32) + branch.astype(F32)).astype(BF16)
            state = jnp.where(layers[index][2], total, state)

    totals = [None] * count
    for index in reversed(range(count)):
        w = weights[index]
        state, inner_one, upper, hidden, inner_two = saved[index]
        grad_c = trade(grad)
        grad_a = trade(apply_back(w[3], grad_c))
        parts = [outer(hidden, grad_a), outer(inner_two, grad_c)]
        grad_u = apply_back(w[2], grad_a) * gelu_slope(upper.astype(F32))
        grad_c = trade(grad_u)
        grad_a = trade(apply_back(w[1], grad_c))
        parts = [outer(state, grad_a), outer(inner_one, grad_c)] + parts
        totals[index] = collect(plan, jnp.stack(parts), half)
        total = (apply_back(w[0], grad_a) + grad.astype(F32)).astype(BF16)
        grad = jnp.where(layers[index][2], total, grad)

    outs = []
    for at in range(4):
        rows = []
        for place in range(slots):
            total = jnp.zeros(factors[0].shape[1:], F32)
            for index, (owner, slot, active) in enumerate(layers):
                here = active & (owner == segment) & (slot == place)
                total = jnp.where(here, totals[index][at], total)
            rows.append(total)
        outs.append(jnp.stack(rows))
    return tuple(outs)


def shards(inputs, first_right, first_left, second_right, second_left, cotangent, sections):
    segments = lax.axis_size("segment")
    devices = lax.axis_size("blk")
    plan = Plan(segments, devices, inputs.shape[0], inputs.shape[2], inputs.shape[3])
    factors = (first_right, first_left, second_right, second_left)
    run = two_segments if plan.kernels else many_segments
    return run(plan, inputs, factors, cotangent, sections)


def solution(mesh):
    whole = P("segment", "blk", None, None)
    tokens = P(None, "blk", None, None)
    in_specs = (tokens, whole, whole, whole, whole, tokens, P())
    return jax.shard_map(
        shards, mesh=mesh, in_specs=in_specs, out_specs=(whole,) * 4, check_vma=False
    )
```

```python
import functools
import math

import jax
import jax.numpy as jnp
from jax import lax
from jax.experimental import pallas as pl
from jax.experimental.pallas import tpu as pltpu
from jax.sharding import PartitionSpec as P

F32 = jnp.float32
BF16 = jnp.bfloat16
ROOT = math.sqrt(2.0 / math.pi)


def gelu(u):
    return 0.5 * u * (1.0 + jnp.tanh(ROOT * (u + 0.044715 * (u * u * u))))


def gelu_slope(u):
    square = u * u
    th = jnp.tanh(ROOT * (u + 0.044715 * (u * square)))
    inner = ROOT * (1.0 + 3 * 0.044715 * square)
    return 0.5 * (1.0 + th) + 0.5 * u * (1.0 - th * th) * inner


class Plan:
    def __init__(self, segments, devices, micros, blocks, tokens):
        self.segments = segments
        self.devices = devices
        self.halves = 2 if micros * tokens >= 256 * segments and devices % 2 == 0 else 1
        self.group = devices // self.halves
        self.own = blocks // devices
        self.held = self.own * self.halves
        self.size = blocks
        self.tokens = micros * tokens // (segments * self.halves)
        self.kernels = segments == 2 and micros == 2 and self.own == 8 and tokens % 128 == 0
        self.groups = None
        if self.halves > 1:
            self.groups = [
                [half * self.group + rank for rank in range(self.group)]
                for half in range(self.halves)
            ]

    def packed_shape(self):
        return (self.group, self.held, self.held, self.tokens)

    def natural_shape(self):
        return (self.held, self.size, self.tokens)

    def pack(self, values):
        split = values.reshape(self.held, self.halves, self.group, self.own, self.tokens)
        return split.transpose(2, 1, 3, 0, 4).reshape(self.packed_shape())

    def unpack(self, packed):
        split = packed.reshape(self.group, self.held, self.halves, self.own, self.tokens)
        return split.transpose(1, 2, 0, 3, 4).reshape(self.natural_shape())

    def exchange(self, packed):
        return lax.all_to_all(packed, "blk", 0, 0, axis_index_groups=self.groups, tiled=True)

    def swap_halves(self, value):
        return lax.ppermute(
            value, "blk", [(at, (at + self.group) % self.devices) for at in range(self.devices)]
        )


def matmul(a, b, over_a, over_b):
    return lax.dot_general(a, b, (((over_a,), (over_b,)), ((), ())), preferred_element_type=F32)


def read(plan, ref, at):
    pair = slice(at // 2 * 2 * plan.own, (at // 2 + 1) * 2 * plan.own)
    rows = ref[:, pair].astype(F32)[:, at % 2 * plan.own : (at % 2 + 1) * plan.own]
    return rows.reshape(plan.size, rows.shape[-1])


def start_work(plan, at, scatter, weight, gradient, state):
    scatter(matmul(weight, state[at], 0, 0))


def residual_work(plan, at, scatter, weight, gradient, branch, state, result):
    total = (state[at].astype(F32) + read(plan, branch, at)).astype(BF16)
    result[at] = total
    scatter(matmul(weight, total, 0, 0))


def left_work(plan, at, scatter, weight, gradient, values):
    scatter(matmul(weight, read(plan, values, at).astype(BF16), 0, 0))


def gelu_work(plan, at, scatter, weight, gradient, values):
    scatter(matmul(weight, gelu(read(plan, values, at)).astype(BF16), 0, 0))


def pack_work(plan, at, scatter, weight, gradient, values):
    scatter(values[at].astype(F32))


def last_back_left_work(plan, at, scatter, weight, gradient, grad):
    scatter(matmul(weight, read(plan, grad, at).astype(BF16), 1, 0))


def last_outer_work(plan, at, scatter, weight, gradient, grad, values):
    natural = read(plan, grad, at).astype(BF16)
    gradient(matmul(read(plan, values, at).astype(BF16), natural, 1, 1))


def back_left_work(plan, at, scatter, weight, gradient, grad, values):
    natural = read(plan, grad, at).astype(BF16)
    scatter(matmul(weight, natural, 1, 0))
    gradient(matmul(read(plan, values, at).astype(BF16), natural, 1, 1))


def back_gelu_work(plan, at, scatter, weight, gradient, grad, values):
    natural = read(plan, grad, at).astype(BF16)
    upper = read(plan, values, at)
    scatter(matmul(weight, natural, 1, 0) * gelu_slope(upper))
    gradient(matmul(gelu(upper).astype(BF16), natural, 1, 1))


def back_right_work(plan, at, scatter, weight, gradient, grad, state, above, result):
    natural = read(plan, grad, at).astype(BF16)
    total = matmul(weight, natural, 1, 0) + above[at].astype(F32)
    result[at] = total.astype(BF16)
    scatter(total)
    gradient(matmul(state[at], natural, 1, 1))


def end_work(plan, at, scatter, weight, gradient, grad, state):
    natural = read(plan, grad, at).astype(BF16)
    gradient(matmul(state[at], natural, 1, 1))


class Kernels:
    def __init__(self, plan, tokens, picks):
        self.plan = plan
        self.picks = picks
        self.tokens = tokens
        self.natural = (plan.own, plan.size, tokens)
        self.sent = (plan.devices, plan.own * plan.own, tokens)
        self.square = (plan.own, plan.size, plan.size)

    def run(
        self, work, ins, packed=0, weight=None, send=True, naturals=0, grads=False, after=(), join=None
    ):
        plan, tokens, picks = self.plan, self.tokens, self.picks
        rows = plan.own * plan.own

        def whole(shape):
            return pl.BlockSpec(shape, lambda turn, picks: (0,) * len(shape))

        def one_part(part):
            return pl.BlockSpec((plan.devices, rows, tokens), lambda turn, picks: (0, part, 0))

        natural, square = whole(self.natural), whole(self.square)
        operands, in_specs = [], []
        for at, value in enumerate(ins):
            value, part = value if isinstance(value, tuple) else (value, 0)
            operands.append(value)
            in_specs.append(one_part(part) if at < packed else natural)
        layer, mine, theirs = weight or (0, None, None)
        matrices = [m for m in (mine, theirs) if m is not None]
        for matrix in matrices:
            operands.append(matrix)
            if len(matrix.shape) == 4:
                block = (None,) + self.square
                in_specs.append(pl.BlockSpec(block, lambda turn, picks: (picks[2 * layer], 0, 0, 0)))
            else:
                in_specs.append(square)
        unread = list(after) + ([] if join is None else [join])
        operands += unread
        in_specs += [pl.BlockSpec(memory_space=pl.ANY)] * len(unread)
        aliases = {} if join is None else {len(operands): 0}
        outs, out_specs, scratch = [], [], []
        if send is True:
            outs.append(jax.ShapeDtypeStruct(self.sent, BF16))
            out_specs.append(one_part(0))
        elif send is not None:
            outs.append(jax.ShapeDtypeStruct((plan.devices, 2 * rows, tokens), BF16))
            out_specs.append(one_part(send))
        if send is not None:
            scratch.append(pltpu.VMEM((tokens // 128, plan.size * plan.own, 128), F32))
        outs += [jax.ShapeDtypeStruct(self.natural, BF16)] * naturals
        out_specs += [natural] * naturals
        if grads:
            outs.append(jax.ShapeDtypeStruct(self.square, BF16))
            out_specs.append(square)

        def kernel(picks, *refs):
            refs = list(refs)
            inner = [refs.pop(0) for i in ins]
            factors = [refs.pop(0) for i in matrices]
            del refs[: len(unread)]
            out = refs.pop(0) if send is not None else None
            inner += [refs.pop(0) for i in range(naturals)]
            gradients = [refs.pop(0)] if grads else []
            store = refs[0] if send is not None else None

            def scatter(at, values):
                spread = pl.ds(at, plan.size, stride=plan.own)
                for part in range(tokens // 128):
                    store[part, spread, :] = values[:, part * 128 : (part + 1) * 128]

            def gradient(at, values):
                for ref in gradients:
                    ref[at] = values.astype(ref.dtype)

            here = picks[2 * layer + 1] == 1
            for at in range(plan.own):
                matrix = None
                if len(factors) == 2:
                    matrix = jnp.where(here, factors[0][at], factors[1][at])
                elif factors:
                    matrix = factors[0][at]
                put = functools.partial(scatter, at)
                work(plan, at, put, matrix, functools.partial(gradient, at), *inner)
            if send is not None:
                for part in range(tokens // 128):
                    values = store[part].astype(BF16).reshape(plan.devices, rows, 128)
                    out[:, :, part * 128 : (part + 1) * 128] = values

        volume = sum(math.prod(o.shape) * o.dtype.itemsize for o in operands + outs)
        products = (1 if matrices else 0) + (1 if grads else 0)
        flops = products * 2 * plan.own * plan.size * plan.size * tokens
        return pl.pallas_call(
            kernel,
            out_shape=outs,
            grid_spec=pltpu.PrefetchScalarGridSpec(
                num_scalar_prefetch=1,
                grid=(1,),
                in_specs=in_specs,
                out_specs=out_specs,
                scratch_shapes=scratch,
            ),
            input_output_aliases=aliases,
            compiler_params=pltpu.CompilerParams(
                vmem_limit_bytes=60 * 1024 * 1024, dimension_semantics=("arbitrary",)
            ),
            cost_estimate=pl.CostEstimate(flops=flops, bytes_accessed=volume, transcendentals=0),
            name=work.__name__,
        )(picks, *operands)


def two_segments(plan, inputs, factors, cotangent, sections):
    segment = lax.axis_index("segment")
    both = [(0, 1), (1, 0)]
    count = 3

    owners = [jnp.int32(0), 2 - sections[0], jnp.int32(1)]
    slots = [jnp.int32(0), sections[0] - 1, sections[1] - 1]
    picks = []
    for owner, slot in zip(owners, slots):
        picks += [jnp.clip(slot, 0, 1), (owner == segment).astype(jnp.int32)]
    kernels = Kernels(plan, inputs.shape[3], jnp.stack(picks).astype(jnp.int32))
    run = kernels.run

    def exchange(value):
        return lax.all_to_all(value, "blk", 0, 0, tiled=True)

    micro = lax.dynamic_index_in_dim(inputs, segment, 0, keepdims=False)
    grad = lax.dynamic_index_in_dim(cotangent, segment, 0, keepdims=False)
    early = lax.ppermute(factors[0][0], "segment", [(0, 1)])
    early = jnp.where(segment == 0, factors[0][0], early)
    received = [lax.ppermute(factor, "segment", both) for factor in factors]

    def weight(layer, at):
        if layer == 0 and at == 0:
            return layer, early, None
        return layer, factors[at], received[at]

    waiting = [(), ()]
    parts = [[None] * 4 for layer in range(count)]

    def step(layer, at, work, ins, packed=2, naturals=0, plain=False, **options):
        use = None if plain else weight(layer, at)
        after = waiting.pop(0) if waiting and not plain else ()
        results = run(work, ins, packed, use, naturals=naturals, grads=True, after=after, **options)
        *results, leave = results
        other = lax.ppermute(leave, "segment", [(1, 0)] if layer == 0 else both)
        if not plain:
            waiting.append((other,))
        parts[layer][at] = (leave, other)
        return results

    saved = []
    state = micro
    sent = run(start_work, (state,), 0, weight(0, 0))[0]
    inner = exchange(sent)
    upper = exchange(run(left_work, (inner,), 1, weight(0, 1))[0])
    inner_two = exchange(run(gelu_work, (upper,), 1, weight(0, 2))[0])
    branch = exchange(run(left_work, (inner_two,), 1, weight(0, 3))[0])
    saved.append((state, inner, upper, inner_two))

    beside = run(pack_work, (grad,), send=1)[0]
    ins = (branch, state)
    sent, state = run(residual_work, ins, 1, weight(1, 0), send=0, naturals=1, join=beside)
    values = exchange(sent)
    inner, last_grad_c = (values, 0), (values, 1)
    upper = exchange(run(left_work, (inner,), 1, weight(1, 1))[0])
    beside = run(last_back_left_work, (last_grad_c,), 1, weight(2, 3), send=1)[0]
    values = exchange(run(gelu_work, (upper,), 1, weight(1, 2), send=0, join=beside)[0])
    inner_two, last_grad_a = (values, 0), (values, 1)
    branch = exchange(run(left_work, (inner_two,), 1, weight(1, 3))[0])
    saved.append((state, inner, upper, inner_two))

    sent, state = run(residual_work, (branch, state), 1, weight(2, 0), naturals=1)
    inner = exchange(sent)
    upper = exchange(run(left_work, (inner,), 1, weight(2, 1))[0])

    sent = step(2, 2, back_gelu_work, (last_grad_a, upper))[0]
    beside = run(gelu_work, (upper,), 1, weight(2, 2), send=1)[0]
    sent = step(2, 1, back_left_work, (exchange(sent), inner), send=0, join=beside)[0]
    values = exchange(sent)
    grad_a, inner_two = (values, 0), (values, 1)
    sent, grad = step(2, 0, back_right_work, (grad_a, state, grad), 1, 1)
    step(2, 3, last_outer_work, (last_grad_c, inner_two), plain=True, send=None)
    for layer in (1, 0):
        state, inner, upper, inner_two = saved[layer]
        sent = step(layer, 3, back_left_work, (exchange(sent), inner_two))[0]
        sent = step(layer, 2, back_gelu_work, (exchange(sent), upper))[0]
        sent = step(layer, 1, back_left_work, (exchange(sent), inner))[0]
        if layer > 0:
            ins = (exchange(sent), state, grad)
            sent, grad = step(layer, 0, back_right_work, ins, 1, 1)
    step(0, 0, end_work, (exchange(sent), state), 1, plain=True, send=None)

    outs = []
    first_has_two = sections[0] == 2
    for at in range(4):
        zero, one, two = [
            stay.astype(F32) + other.astype(F32) for stay, other in (p[at] for p in parts)
        ]
        low = jnp.where(segment == 0, zero, jnp.where(first_has_two, two, one))
        high = jnp.where(segment == 0, one, two)
        high = jnp.where(first_has_two == (segment == 0), high, 0.0)
        outs.append(jnp.stack([low, high]))
    return tuple(outs)


def apply(weight, values):
    return jnp.einsum("bij,bit->bjt", weight, values, preferred_element_type=F32)


def apply_back(weight, values):
    return jnp.einsum("bij,bjt->bit", weight, values, preferred_element_type=F32)


def outer(values, grad):
    return jnp.einsum("bit,bjt->bij", values, grad, preferred_element_type=F32).astype(BF16)


def spread(plan, factor, owner, half):
    every = lax.all_gather(factor, "segment", axis=0)
    factor = lax.dynamic_index_in_dim(every, owner, 0, keepdims=False)
    if plan.halves == 1:
        return factor
    other = plan.swap_halves(factor)
    lower = jnp.where(half == 0, factor, other)
    upper = jnp.where(half == 0, other, factor)
    return jnp.concatenate([lower, upper], axis=1)


def collect(plan, parts, half):
    if plan.halves == 1:
        return lax.psum(parts.astype(F32), "segment")
    lower, upper = parts[:, : plan.own], parts[:, plan.own :]
    kept = jnp.where(half == 0, lower, upper)
    other = plan.swap_halves(jnp.where(half == 0, upper, lower))
    return lax.psum(kept.astype(F32) + other.astype(F32), "segment")


def token_chunk(plan, values, half):
    mine = lax.axis_index("segment")
    per_micro = values.shape[-1] // plan.tokens

    def chunk(at):
        at = mine * plan.halves + at
        micro = lax.dynamic_index_in_dim(values, at // per_micro, 0, keepdims=False)
        start = (at % per_micro) * plan.tokens
        return lax.dynamic_slice_in_dim(micro, start, plan.tokens, 2)

    if plan.halves == 1:
        return chunk(0)
    kept, other = chunk(half), plan.swap_halves(chunk(1 - half))
    lower = jnp.where(half == 0, kept, other)
    upper = jnp.where(half == 0, other, kept)
    return jnp.concatenate([lower, upper], axis=0)


def many_segments(plan, inputs, factors, cotangent, sections):
    segment = lax.axis_index("segment")
    half = lax.axis_index("blk") // plan.group
    slots = factors[0].shape[0]

    def trade(values):
        return plan.unpack(plan.exchange(plan.pack(values.astype(BF16))))

    count = plan.segments * slots - 1
    ends = jnp.cumsum(sections)
    layers, weights = [], []
    for index in range(count):
        owner = jnp.minimum(jnp.sum((index >= ends).astype(jnp.int32)), plan.segments - 1)
        slot = jnp.clip(index - (ends[owner] - sections[owner]), 0, slots - 1)
        layers.append((owner, slot, index < ends[-1]))
        picked = [lax.dynamic_index_in_dim(f, slot, 0, keepdims=True) for f in factors]
        weights.append(spread(plan, jnp.concatenate(picked, axis=0), owner, half))

    state = token_chunk(plan, inputs, half)
    grad = token_chunk(plan, cotangent, half)
    saved = []
    for index in range(count):
        w = weights[index]
        inner_one = trade(apply(w[0], state))
        upper = trade(apply(w[1], inner_one))
        hidden = gelu(upper.astype(F32)).astype(BF16)
        inner_two = trade(apply(w[2], hidden))
        saved.append((state, inner_one, upper, hidden, inner_two))
        if index < count - 1:
            branch = trade(apply(w[3], inner_two))
            total = (state.astype(F32) + branch.astype(F32)).astype(BF16)
            state = jnp.where(layers[index][2], total, state)

    totals = [None] * count
    for index in reversed(range(count)):
        w = weights[index]
        state, inner_one, upper, hidden, inner_two = saved[index]
        grad_c = trade(grad)
        grad_a = trade(apply_back(w[3], grad_c))
        parts = [outer(hidden, grad_a), outer(inner_two, grad_c)]
        grad_u = apply_back(w[2], grad_a) * gelu_slope(upper.astype(F32))
        grad_c = trade(grad_u)
        grad_a = trade(apply_back(w[1], grad_c))
        parts = [outer(state, grad_a), outer(inner_one, grad_c)] + parts
        totals[index] = collect(plan, jnp.stack(parts), half)
        total = (apply_back(w[0], grad_a) + grad.astype(F32)).astype(BF16)
        grad = jnp.where(layers[index][2], total, grad)

    outs = []
    for at in range(4):
        rows = []
        for place in range(slots):
            total = jnp.zeros(factors[0].shape[1:], F32)
            for index, (owner, slot, active) in enumerate(layers):
                here = active & (owner == segment) & (slot == place)
                total = jnp.where(here, totals[index][at], total)
            rows.append(total)
        outs.append(jnp.stack(rows))
    return tuple(outs)


def shards(inputs, first_right, first_left, second_right, second_left, cotangent, sections):
    segments = lax.axis_size("segment")
    devices = lax.axis_size("blk")
    plan = Plan(segments, devices, inputs.shape[0], inputs.shape[2], inputs.shape[3])
    factors = (first_right, first_left, second_right, second_left)
    run = two_segments if plan.kernels else many_segments
    return run(plan, inputs, factors, cotangent, sections)


def solution(mesh):
    whole = P("segment", "blk", None, None)
    tokens = P(None, "blk", None, None)
    in_specs = (tokens, whole, whole, whole, whole, tokens, P())
    return jax.shard_map(
        shards, mesh=mesh, in_specs=in_specs, out_specs=(whole,) * 4, check_vma=False
    )
```

```python
import functools
import math

import jax
import jax.numpy as jnp
from jax import lax
from jax.experimental import pallas as pl
from jax.experimental.pallas import tpu as pltpu
from jax.sharding import PartitionSpec as P

F32 = jnp.float32
BF16 = jnp.bfloat16
ROOT = math.sqrt(2.0 / math.pi)


def gelu(u):
    return 0.5 * u * (1.0 + jnp.tanh(ROOT * (u + 0.044715 * (u * u * u))))


def gelu_slope(u):
    square = u * u
    th = jnp.tanh(ROOT * (u + 0.044715 * (u * square)))
    inner = ROOT * (1.0 + 3 * 0.044715 * square)
    return 0.5 * (1.0 + th) + 0.5 * u * (1.0 - th * th) * inner


class Plan:
    def __init__(self, segments, devices, micros, blocks, tokens):
        self.segments = segments
        self.devices = devices
        self.halves = 2 if micros * tokens >= 256 * segments and devices % 2 == 0 else 1
        self.group = devices // self.halves
        self.own = blocks // devices
        self.held = self.own * self.halves
        self.size = blocks
        self.tokens = micros * tokens // (segments * self.halves)
        self.kernels = segments == 2 and micros == 2 and self.own == 8 and tokens % 128 == 0
        self.groups = None
        if self.halves > 1:
            self.groups = [
                [half * self.group + rank for rank in range(self.group)]
                for half in range(self.halves)
            ]

    def packed_shape(self):
        return (self.group, self.held, self.held, self.tokens)

    def natural_shape(self):
        return (self.held, self.size, self.tokens)

    def pack(self, values):
        split = values.reshape(self.held, self.halves, self.group, self.own, self.tokens)
        return split.transpose(2, 1, 3, 0, 4).reshape(self.packed_shape())

    def unpack(self, packed):
        split = packed.reshape(self.group, self.held, self.halves, self.own, self.tokens)
        return split.transpose(1, 2, 0, 3, 4).reshape(self.natural_shape())

    def exchange(self, packed):
        return lax.all_to_all(packed, "blk", 0, 0, axis_index_groups=self.groups, tiled=True)

    def swap_halves(self, value):
        return lax.ppermute(
            value, "blk", [(at, (at + self.group) % self.devices) for at in range(self.devices)]
        )


def matmul(a, b, over_a, over_b):
    return lax.dot_general(a, b, (((over_a,), (over_b,)), ((), ())), preferred_element_type=F32)


def read(plan, ref, at):
    pair = slice(at // 2 * 2 * plan.own, (at // 2 + 1) * 2 * plan.own)
    rows = ref[:, pair].astype(F32)[:, at % 2 * plan.own : (at % 2 + 1) * plan.own]
    return rows.reshape(plan.size, rows.shape[-1])


def start_work(plan, at, scatter, weight, gradient, state):
    scatter(matmul(weight, state[at], 0, 0))


def residual_work(plan, at, scatter, weight, gradient, branch, state, result):
    total = (state[at].astype(F32) + read(plan, branch, at)).astype(BF16)
    result[at] = total
    scatter(matmul(weight, total, 0, 0))


def left_work(plan, at, scatter, weight, gradient, values):
    scatter(matmul(weight, read(plan, values, at).astype(BF16), 0, 0))


def gelu_work(plan, at, scatter, weight, gradient, values):
    scatter(matmul(weight, gelu(read(plan, values, at)).astype(BF16), 0, 0))


def pack_work(plan, at, scatter, weight, gradient, values):
    scatter(values[at].astype(F32))


def last_back_left_work(plan, at, scatter, weight, gradient, grad):
    scatter(matmul(weight, read(plan, grad, at).astype(BF16), 1, 0))


def last_outer_work(plan, at, scatter, weight, gradient, grad, values):
    natural = read(plan, grad, at).astype(BF16)
    gradient(matmul(read(plan, values, at).astype(BF16), natural, 1, 1))


def back_left_work(plan, at, scatter, weight, gradient, grad, values):
    natural = read(plan, grad, at).astype(BF16)
    scatter(matmul(weight, natural, 1, 0))
    gradient(matmul(read(plan, values, at).astype(BF16), natural, 1, 1))


def back_gelu_work(plan, at, scatter, weight, gradient, grad, values):
    natural = read(plan, grad, at).astype(BF16)
    upper = read(plan, values, at)
    scatter(matmul(weight, natural, 1, 0) * gelu_slope(upper))
    gradient(matmul(gelu(upper).astype(BF16), natural, 1, 1))


def back_right_work(plan, at, scatter, weight, gradient, grad, state, above, result):
    natural = read(plan, grad, at).astype(BF16)
    total = matmul(weight, natural, 1, 0) + above[at].astype(F32)
    result[at] = total.astype(BF16)
    scatter(total)
    gradient(matmul(state[at], natural, 1, 1))


def end_work(plan, at, scatter, weight, gradient, grad, state):
    natural = read(plan, grad, at).astype(BF16)
    gradient(matmul(state[at], natural, 1, 1))


class Kernels:
    def __init__(self, plan, tokens, picks):
        self.plan = plan
        self.picks = picks
        self.tokens = tokens
        self.natural = (plan.own, plan.size, tokens)
        self.sent = (plan.devices, plan.own * plan.own, tokens)
        self.square = (plan.own, plan.size, plan.size)

    def run(
        self, work, ins, packed=0, weight=None, send=True, naturals=0, grads=False, after=(), join=None
    ):
        plan, tokens, picks = self.plan, self.tokens, self.picks
        rows = plan.own * plan.own
        pieces = 2
        span = plan.own // pieces
        arrays = [value[0] if isinstance(value, tuple) else value for value in ins]
        places = [value[1] if isinstance(value, tuple) else 0 for value in ins]
        direct = 1 if packed else 0
        layer, mine, theirs = weight or (0, None, None)
        matrices = [m for m in (mine, theirs) if m is not None]
        unread = list(after) + ([] if join is None else [join])
        operands = arrays + matrices + unread
        aliases = {} if join is None else {len(operands): 0}
        outs = []
        if send is not None:
            parts = 1 if send is True else 2
            outs.append(jax.ShapeDtypeStruct((plan.devices, parts * rows, tokens), BF16))
        outs += [jax.ShapeDtypeStruct(self.natural, BF16)] * naturals
        outs += [jax.ShapeDtypeStruct(self.square, BF16)] * (1 if grads else 0)
        blocks = outs[0 if send is None else 1 :]
        scratch = [pltpu.VMEM(self.sent, BF16)] * (packed - direct)
        scratch += [pltpu.VMEM(self.natural, BF16)] * (len(ins) - packed)
        scratch += [pltpu.VMEM(self.square, BF16)] * (1 if matrices else 0)
        scratch += [pltpu.VMEM(block.shape, block.dtype) for block in blocks]
        if send is not None:
            scratch.append(pltpu.VMEM(self.sent, BF16))
            scratch.append(pltpu.VMEM((tokens // 128, plan.size * plan.own, 128), F32))
        scratch.append(pltpu.SemaphoreType.DMA((len(ins) + 1, pieces)))
        scratch.append(pltpu.SemaphoreType.DMA((len(outs) + 1, pieces)))

        def kernel(picks, *refs):
            refs = list(refs)

            def take(count):
                return [refs.pop(0) for i in range(count)]

            sources, factors = take(len(ins)), take(len(matrices))
            take(len(unread))
            out = take(1)[0] if send is not None else None
            targets = take(len(blocks))
            inner = []
            if direct:
                inner.append(sources[0].at[:, pl.ds(places[0] * rows, rows)])
            inner += take(len(ins) - direct)
            matrix = take(1)[0] if matrices else None
            results = take(len(blocks))
            ready, store = take(2) if send is not None else (None, None)
            in_sems, out_sems = take(2)
            here = picks[2 * layer + 1] == 1

            def arrival(at, piece):
                source, target = sources[at], inner[at]
                if at < packed:
                    width = span * plan.own
                    source = source.at[:, pl.ds(places[at] * rows + piece * width, width)]
                    target = target.at[:, pl.ds(piece * width, width)]
                else:
                    source = source.at[pl.ds(piece * span, span)]
                    target = target.at[pl.ds(piece * span, span)]
                return pltpu.make_async_copy(source, target, in_sems.at[at, piece])

            def factor(which, piece):
                source = factors[which]
                if len(source.shape) == 4:
                    source = source.at[picks[2 * layer]]
                part = pl.ds(piece * span, span)
                sem = in_sems.at[len(ins), piece]
                return pltpu.make_async_copy(source.at[part], matrix.at[part], sem)

            def departure(at, piece):
                part = pl.ds(piece * span, span)
                sem = out_sems.at[at, piece]
                return pltpu.make_async_copy(results[at].at[part], targets[at].at[part], sem)

            width = plan.devices // pieces

            def sending(piece):
                part = pl.ds(piece * width, width)
                first = 0 if send is True else send * rows
                target = out.at[part, pl.ds(first, rows)]
                sem = out_sems.at[len(outs), piece]
                return pltpu.make_async_copy(ready.at[part], target, sem)

            for piece in range(pieces):
                if len(factors) == 2:

                    @pl.when(here)
                    def _():
                        factor(0, piece).start()

                    @pl.when(jnp.logical_not(here))
                    def _():
                        factor(1, piece).start()

                elif factors:
                    factor(0, piece).start()
                for at in range(direct, len(ins)):
                    arrival(at, piece).start()

            def scatter(at, values):
                spread = pl.ds(at, plan.size, stride=plan.own)
                for part in range(tokens // 128):
                    store[part, spread, :] = values[:, part * 128 : (part + 1) * 128]

            def gradient(at, values):
                for ref in results[naturals:]:
                    ref[at] = values.astype(ref.dtype)

            for at in range(plan.own):
                piece = at // span
                if at % span == 0:
                    if factors:
                        factor(0, piece).wait()
                    for place in range(direct, len(ins)):
                        arrival(place, piece).wait()
                put = functools.partial(scatter, at)
                used = matrix[at] if factors else None
                refs_of_work = inner + results[:naturals]
                work(plan, at, put, used, functools.partial(gradient, at), *refs_of_work)
                if at % span == span - 1:
                    for place in range(len(blocks)):
                        departure(place, piece).start()
            for piece in range(pieces):
                if send is None:
                    break
                part = slice(piece * width, (piece + 1) * width)
                for chunk in range(tokens // 128):
                    values = store[chunk, part.start * rows : part.stop * rows].astype(BF16)
                    lanes = slice(chunk * 128, (chunk + 1) * 128)
                    ready[part, :, lanes] = values.reshape(width, rows, 128)
                sending(piece).start()
            for piece in range(pieces):
                for place in range(len(blocks)):
                    departure(place, piece).wait()
                if send is not None:
                    sending(piece).wait()

        anywhere = pl.BlockSpec(memory_space=pl.ANY)
        here_already = [pl.BlockSpec(memory_space=pltpu.VMEM)] * direct
        volume = sum(math.prod(o.shape) * o.dtype.itemsize for o in operands + outs)
        products = (1 if matrices else 0) + (1 if grads else 0)
        flops = products * 2 * plan.own * plan.size * plan.size * tokens
        return pl.pallas_call(
            kernel,
            out_shape=outs,
            in_specs=[pl.BlockSpec(memory_space=pltpu.SMEM)]
            + here_already
            + [anywhere] * (len(operands) - direct),
            out_specs=[anywhere] * len(outs),
            scratch_shapes=scratch,
            input_output_aliases=aliases,
            compiler_params=pltpu.CompilerParams(vmem_limit_bytes=52 * 1024 * 1024),
            cost_estimate=pl.CostEstimate(flops=flops, bytes_accessed=volume, transcendentals=0),
            name=work.__name__,
        )(picks, *operands)


def two_segments(plan, inputs, factors, cotangent, sections):
    segment = lax.axis_index("segment")
    both = [(0, 1), (1, 0)]
    count = 3

    owners = [jnp.int32(0), 2 - sections[0], jnp.int32(1)]
    slots = [jnp.int32(0), sections[0] - 1, sections[1] - 1]
    picks = []
    for owner, slot in zip(owners, slots):
        picks += [jnp.clip(slot, 0, 1), (owner == segment).astype(jnp.int32)]
    kernels = Kernels(plan, inputs.shape[3], jnp.stack(picks).astype(jnp.int32))
    run = kernels.run

    def exchange(value):
        return lax.all_to_all(value, "blk", 0, 0, tiled=True)

    micro = lax.dynamic_index_in_dim(inputs, segment, 0, keepdims=False)
    grad = lax.dynamic_index_in_dim(cotangent, segment, 0, keepdims=False)
    early = lax.ppermute(factors[0][0], "segment", [(0, 1)])
    early = jnp.where(segment == 0, factors[0][0], early)
    received = [lax.ppermute(factor, "segment", both) for factor in factors]

    def weight(layer, at):
        if layer == 0 and at == 0:
            return layer, early, None
        return layer, factors[at], received[at]

    waiting = [(), ()]
    parts = [[None] * 4 for layer in range(count)]

    def step(layer, at, work, ins, packed=2, naturals=0, plain=False, **options):
        use = None if plain else weight(layer, at)
        after = waiting.pop(0) if waiting and not plain else ()
        results = run(work, ins, packed, use, naturals=naturals, grads=True, after=after, **options)
        *results, leave = results
        other = lax.ppermute(leave, "segment", [(1, 0)] if layer == 0 else both)
        if not plain:
            waiting.append((other,))
        parts[layer][at] = (leave, other)
        return results

    saved = []
    state = micro
    sent = run(start_work, (state,), 0, weight(0, 0))[0]
    inner = exchange(sent)
    upper = exchange(run(left_work, (inner,), 1, weight(0, 1))[0])
    inner_two = exchange(run(gelu_work, (upper,), 1, weight(0, 2))[0])
    branch = exchange(run(left_work, (inner_two,), 1, weight(0, 3))[0])
    saved.append((state, inner, upper, inner_two))

    beside = run(pack_work, (grad,), send=1)[0]
    ins = (branch, state)
    sent, state = run(residual_work, ins, 1, weight(1, 0), send=0, naturals=1, join=beside)
    values = exchange(sent)
    inner, last_grad_c = (values, 0), (values, 1)
    upper = exchange(run(left_work, (inner,), 1, weight(1, 1))[0])
    beside = run(last_back_left_work, (last_grad_c,), 1, weight(2, 3), send=1)[0]
    values = exchange(run(gelu_work, (upper,), 1, weight(1, 2), send=0, join=beside)[0])
    inner_two, last_grad_a = (values, 0), (values, 1)
    branch = exchange(run(left_work, (inner_two,), 1, weight(1, 3))[0])
    saved.append((state, inner, upper, inner_two))

    sent, state = run(residual_work, (branch, state), 1, weight(2, 0), naturals=1)
    inner = exchange(sent)
    upper = exchange(run(left_work, (inner,), 1, weight(2, 1))[0])

    sent = step(2, 2, back_gelu_work, (last_grad_a, upper))[0]
    beside = run(gelu_work, (upper,), 1, weight(2, 2), send=1)[0]
    sent = step(2, 1, back_left_work, (exchange(sent), inner), send=0, join=beside)[0]
    values = exchange(sent)
    grad_a, inner_two = (values, 0), (values, 1)
    sent, grad = step(2, 0, back_right_work, (grad_a, state, grad), 1, 1)
    step(2, 3, last_outer_work, (last_grad_c, inner_two), plain=True, send=None)
    for layer in (1, 0):
        state, inner, upper, inner_two = saved[layer]
        sent = step(layer, 3, back_left_work, (exchange(sent), inner_two))[0]
        sent = step(layer, 2, back_gelu_work, (exchange(sent), upper))[0]
        sent = step(layer, 1, back_left_work, (exchange(sent), inner))[0]
        if layer > 0:
            ins = (exchange(sent), state, grad)
            sent, grad = step(layer, 0, back_right_work, ins, 1, 1)
    step(0, 0, end_work, (exchange(sent), state), 1, plain=True, send=None)

    outs = []
    first_has_two = sections[0] == 2
    for at in range(4):
        zero, one, two = [
            stay.astype(F32) + other.astype(F32) for stay, other in (p[at] for p in parts)
        ]
        low = jnp.where(segment == 0, zero, jnp.where(first_has_two, two, one))
        high = jnp.where(segment == 0, one, two)
        high = jnp.where(first_has_two == (segment == 0), high, 0.0)
        outs.append(jnp.stack([low, high]))
    return tuple(outs)


def apply(weight, values):
    return jnp.einsum("bij,bit->bjt", weight, values, preferred_element_type=F32)


def apply_back(weight, values):
    return jnp.einsum("bij,bjt->bit", weight, values, preferred_element_type=F32)


def outer(values, grad):
    return jnp.einsum("bit,bjt->bij", values, grad, preferred_element_type=F32).astype(BF16)


def spread(plan, factor, owner, half):
    every = lax.all_gather(factor, "segment", axis=0)
    factor = lax.dynamic_index_in_dim(every, owner, 0, keepdims=False)
    if plan.halves == 1:
        return factor
    other = plan.swap_halves(factor)
    lower = jnp.where(half == 0, factor, other)
    upper = jnp.where(half == 0, other, factor)
    return jnp.concatenate([lower, upper], axis=1)


def collect(plan, parts, half):
    if plan.halves == 1:
        return lax.psum(parts.astype(F32), "segment")
    lower, upper = parts[:, : plan.own], parts[:, plan.own :]
    kept = jnp.where(half == 0, lower, upper)
    other = plan.swap_halves(jnp.where(half == 0, upper, lower))
    return lax.psum(kept.astype(F32) + other.astype(F32), "segment")


def token_chunk(plan, values, half):
    mine = lax.axis_index("segment")
    per_micro = values.shape[-1] // plan.tokens

    def chunk(at):
        at = mine * plan.halves + at
        micro = lax.dynamic_index_in_dim(values, at // per_micro, 0, keepdims=False)
        start = (at % per_micro) * plan.tokens
        return lax.dynamic_slice_in_dim(micro, start, plan.tokens, 2)

    if plan.halves == 1:
        return chunk(0)
    kept, other = chunk(half), plan.swap_halves(chunk(1 - half))
    lower = jnp.where(half == 0, kept, other)
    upper = jnp.where(half == 0, other, kept)
    return jnp.concatenate([lower, upper], axis=0)


def many_segments(plan, inputs, factors, cotangent, sections):
    segment = lax.axis_index("segment")
    half = lax.axis_index("blk") // plan.group
    slots = factors[0].shape[0]

    def trade(values):
        return plan.unpack(plan.exchange(plan.pack(values.astype(BF16))))

    count = plan.segments * slots - 1
    ends = jnp.cumsum(sections)
    layers, weights = [], []
    for index in range(count):
        owner = jnp.minimum(jnp.sum((index >= ends).astype(jnp.int32)), plan.segments - 1)
        slot = jnp.clip(index - (ends[owner] - sections[owner]), 0, slots - 1)
        layers.append((owner, slot, index < ends[-1]))
        picked = [lax.dynamic_index_in_dim(f, slot, 0, keepdims=True) for f in factors]
        weights.append(spread(plan, jnp.concatenate(picked, axis=0), owner, half))

    state = token_chunk(plan, inputs, half)
    grad = token_chunk(plan, cotangent, half)
    saved = []
    for index in range(count):
        w = weights[index]
        inner_one = trade(apply(w[0], state))
        upper = trade(apply(w[1], inner_one))
        hidden = gelu(upper.astype(F32)).astype(BF16)
        inner_two = trade(apply(w[2], hidden))
        saved.append((state, inner_one, upper, hidden, inner_two))
        if index < count - 1:
            branch = trade(apply(w[3], inner_two))
            total = (state.astype(F32) + branch.astype(F32)).astype(BF16)
            state = jnp.where(layers[index][2], total, state)

    totals = [None] * count
    for index in reversed(range(count)):
        w = weights[index]
        state, inner_one, upper, hidden, inner_two = saved[index]
        grad_c = trade(grad)
        grad_a = trade(apply_back(w[3], grad_c))
        parts = [outer(hidden, grad_a), outer(inner_two, grad_c)]
        grad_u = apply_back(w[2], grad_a) * gelu_slope(upper.astype(F32))
        grad_c = trade(grad_u)
        grad_a = trade(apply_back(w[1], grad_c))
        parts = [outer(state, grad_a), outer(inner_one, grad_c)] + parts
        totals[index] = collect(plan, jnp.stack(parts), half)
        total = (apply_back(w[0], grad_a) + grad.astype(F32)).astype(BF16)
        grad = jnp.where(layers[index][2], total, grad)

    outs = []
    for at in range(4):
        rows = []
        for place in range(slots):
            total = jnp.zeros(factors[0].shape[1:], F32)
            for index, (owner, slot, active) in enumerate(layers):
                here = active & (owner == segment) & (slot == place)
                total = jnp.where(here, totals[index][at], total)
            rows.append(total)
        outs.append(jnp.stack(rows))
    return tuple(outs)


def shards(inputs, first_right, first_left, second_right, second_left, cotangent, sections):
    segments = lax.axis_size("segment")
    devices = lax.axis_size("blk")
    plan = Plan(segments, devices, inputs.shape[0], inputs.shape[2], inputs.shape[3])
    factors = (first_right, first_left, second_right, second_left)
    run = two_segments if plan.kernels else many_segments
    return run(plan, inputs, factors, cotangent, sections)


def solution(mesh):
    whole = P("segment", "blk", None, None)
    tokens = P(None, "blk", None, None)
    in_specs = (tokens, whole, whole, whole, whole, tokens, P())
    return jax.shard_map(
        shards, mesh=mesh, in_specs=in_specs, out_specs=(whole,) * 4, check_vma=False
    )
```

```python
import functools
import math

import jax
import jax.numpy as jnp
from jax import lax
from jax.experimental import pallas as pl
from jax.experimental.pallas import tpu as pltpu
from jax.sharding import PartitionSpec as P

F32 = jnp.float32
BF16 = jnp.bfloat16
ROOT = math.sqrt(2.0 / math.pi)


def gelu(u):
    return 0.5 * u * (1.0 + jnp.tanh(ROOT * (u + 0.044715 * (u * u * u))))


def gelu_slope(u):
    square = u * u
    th = jnp.tanh(ROOT * (u + 0.044715 * (u * square)))
    inner = ROOT * (1.0 + 3 * 0.044715 * square)
    return 0.5 * (1.0 + th) + 0.5 * u * (1.0 - th * th) * inner


class Plan:
    def __init__(self, segments, devices, micros, blocks, tokens):
        self.segments = segments
        self.devices = devices
        self.halves = 2 if micros * tokens >= 256 * segments and devices % 2 == 0 else 1
        self.group = devices // self.halves
        self.own = blocks // devices
        self.held = self.own * self.halves
        self.size = blocks
        self.tokens = micros * tokens // (segments * self.halves)
        self.kernels = segments == 2 and micros == 2 and self.own == 8 and tokens % 128 == 0
        self.groups = None
        if self.halves > 1:
            self.groups = [
                [half * self.group + rank for rank in range(self.group)]
                for half in range(self.halves)
            ]

    def packed_shape(self):
        return (self.group, self.held, self.held, self.tokens)

    def natural_shape(self):
        return (self.held, self.size, self.tokens)

    def pack(self, values):
        split = values.reshape(self.held, self.halves, self.group, self.own, self.tokens)
        return split.transpose(2, 1, 3, 0, 4).reshape(self.packed_shape())

    def unpack(self, packed):
        split = packed.reshape(self.group, self.held, self.halves, self.own, self.tokens)
        return split.transpose(1, 2, 0, 3, 4).reshape(self.natural_shape())

    def exchange(self, packed):
        return lax.all_to_all(packed, "blk", 0, 0, axis_index_groups=self.groups, tiled=True)

    def swap_halves(self, value):
        return lax.ppermute(
            value, "blk", [(at, (at + self.group) % self.devices) for at in range(self.devices)]
        )


def matmul(a, b, over_a, over_b):
    return lax.dot_general(a, b, (((over_a,), (over_b,)), ((), ())), preferred_element_type=F32)


def read(plan, ref, at):
    pair = slice(at // 2 * 2 * plan.own, (at // 2 + 1) * 2 * plan.own)
    rows = ref[:, pair].astype(F32)[:, at % 2 * plan.own : (at % 2 + 1) * plan.own]
    return rows.reshape(plan.size, rows.shape[-1])


def start_work(plan, at, scatter, weight, gradient, state):
    scatter(matmul(weight, state[at], 0, 0))


def residual_work(plan, at, scatter, weight, gradient, branch, state, result):
    total = (state[at].astype(F32) + read(plan, branch, at)).astype(BF16)
    result[at] = total
    scatter(matmul(weight, total, 0, 0))


def left_work(plan, at, scatter, weight, gradient, values):
    scatter(matmul(weight, read(plan, values, at).astype(BF16), 0, 0))


def gelu_work(plan, at, scatter, weight, gradient, values):
    scatter(matmul(weight, gelu(read(plan, values, at)).astype(BF16), 0, 0))


def pack_work(plan, at, scatter, weight, gradient, values):
    scatter(values[at].astype(F32))


def last_back_left_work(plan, at, scatter, weight, gradient, grad):
    scatter(matmul(weight, read(plan, grad, at).astype(BF16), 1, 0))


def last_outer_work(plan, at, scatter, weight, gradient, grad, values):
    natural = read(plan, grad, at).astype(BF16)
    gradient(matmul(read(plan, values, at).astype(BF16), natural, 1, 1))


def back_left_work(plan, at, scatter, weight, gradient, grad, values):
    natural = read(plan, grad, at).astype(BF16)
    scatter(matmul(weight, natural, 1, 0))
    gradient(matmul(read(plan, values, at).astype(BF16), natural, 1, 1))


def back_gelu_work(plan, at, scatter, weight, gradient, grad, values):
    natural = read(plan, grad, at).astype(BF16)
    upper = read(plan, values, at)
    scatter(matmul(weight, natural, 1, 0) * gelu_slope(upper))
    gradient(matmul(gelu(upper).astype(BF16), natural, 1, 1))


def back_right_work(plan, at, scatter, weight, gradient, grad, state, above, result):
    natural = read(plan, grad, at).astype(BF16)
    total = matmul(weight, natural, 1, 0) + above[at].astype(F32)
    result[at] = total.astype(BF16)
    scatter(total)
    gradient(matmul(state[at], natural, 1, 1))


def end_work(plan, at, scatter, weight, gradient, grad, state):
    natural = read(plan, grad, at).astype(BF16)
    gradient(matmul(state[at], natural, 1, 1))


class Kernels:
    def __init__(self, plan, tokens, picks):
        self.plan = plan
        self.picks = picks
        self.tokens = tokens
        self.natural = (plan.own, plan.size, tokens)
        self.sent = (plan.devices, plan.own * plan.own, tokens)
        self.square = (plan.own, plan.size, plan.size)

    def run(
        self, work, ins, packed=0, weight=None, send=True, naturals=0, grads=False, after=(), join=None
    ):
        plan, tokens, picks = self.plan, self.tokens, self.picks
        rows = plan.own * plan.own
        pieces = 2
        span = plan.own // pieces
        arrays = [value[0] if isinstance(value, tuple) else value for value in ins]
        places = [value[1] if isinstance(value, tuple) else 0 for value in ins]
        direct = 1 if packed else 0
        layer, mine, theirs = weight or (0, None, None)
        matrices = [m for m in (mine, theirs) if m is not None]
        unread = list(after) + ([] if join is None else [join])
        operands = arrays + matrices + unread
        aliases = {} if join is None else {len(operands): 0}
        outs = []
        if send is not None:
            parts = 1 if send is True else 2
            outs.append(jax.ShapeDtypeStruct((plan.devices, parts * rows, tokens), BF16))
        outs += [jax.ShapeDtypeStruct(self.natural, BF16)] * naturals
        outs += [jax.ShapeDtypeStruct(self.square, BF16)] * (1 if grads else 0)
        blocks = outs[0 if send is None else 1 :]
        scratch = [pltpu.VMEM(self.sent, BF16)] * (packed - direct)
        scratch += [pltpu.VMEM(self.natural, BF16)] * (len(ins) - packed)
        scratch += [pltpu.VMEM(self.square, BF16)] * (1 if matrices else 0)
        scratch += [pltpu.VMEM(block.shape, block.dtype) for block in blocks]
        if send is not None:
            scratch.append(pltpu.VMEM(self.sent, BF16))
            scratch.append(pltpu.VMEM((tokens // 128, plan.size * plan.own, 128), F32))
        scratch.append(pltpu.SemaphoreType.DMA((len(ins) + 1, pieces)))
        scratch.append(pltpu.SemaphoreType.DMA((len(outs) + 1, pieces)))

        def kernel(picks, *refs):
            refs = list(refs)

            def take(count):
                return [refs.pop(0) for i in range(count)]

            sources, factors = take(len(ins)), take(len(matrices))
            take(len(unread))
            out = take(1)[0] if send is not None else None
            targets = take(len(blocks))
            inner = []
            if direct:
                inner.append(sources[0].at[:, pl.ds(places[0] * rows, rows)])
            inner += take(len(ins) - direct)
            matrix = take(1)[0] if matrices else None
            results = take(len(blocks))
            ready, store = take(2) if send is not None else (None, None)
            in_sems, out_sems = take(2)
            here = picks[2 * layer + 1] == 1

            def arrival(at, piece):
                source, target = sources[at], inner[at]
                if at < packed:
                    width = span * plan.own
                    source = source.at[:, pl.ds(places[at] * rows + piece * width, width)]
                    target = target.at[:, pl.ds(piece * width, width)]
                else:
                    source = source.at[pl.ds(piece * span, span)]
                    target = target.at[pl.ds(piece * span, span)]
                return pltpu.make_async_copy(source, target, in_sems.at[at, piece])

            def factor(which, piece):
                source = factors[which]
                if len(source.shape) == 4:
                    source = source.at[picks[2 * layer]]
                part = pl.ds(piece * span, span)
                sem = in_sems.at[len(ins), piece]
                return pltpu.make_async_copy(source.at[part], matrix.at[part], sem)

            def departure(at, piece):
                part = pl.ds(piece * span, span)
                sem = out_sems.at[at, piece]
                return pltpu.make_async_copy(results[at].at[part], targets[at].at[part], sem)

            width = plan.devices // pieces

            def sending(piece):
                part = pl.ds(piece * width, width)
                first = 0 if send is True else send * rows
                target = out.at[part, pl.ds(first, rows)]
                sem = out_sems.at[len(outs), piece]
                return pltpu.make_async_copy(ready.at[part], target, sem)

            for piece in range(pieces):
                if len(factors) == 2:

                    @pl.when(here)
                    def _():
                        factor(0, piece).start()

                    @pl.when(jnp.logical_not(here))
                    def _():
                        factor(1, piece).start()

                elif factors:
                    factor(0, piece).start()
                for at in range(direct, len(ins)):
                    arrival(at, piece).start()

            def scatter(at, values):
                spread = pl.ds(at, plan.size, stride=plan.own)
                for part in range(tokens // 128):
                    store[part, spread, :] = values[:, part * 128 : (part + 1) * 128]

            def gradient(at, values):
                for ref in results[naturals:]:
                    ref[at] = values.astype(ref.dtype)

            for at in range(plan.own):
                piece = at // span
                if at % span == 0:
                    if factors:
                        factor(0, piece).wait()
                    for place in range(direct, len(ins)):
                        arrival(place, piece).wait()
                put = functools.partial(scatter, at)
                used = matrix[at] if factors else None
                refs_of_work = inner + results[:naturals]
                work(plan, at, put, used, functools.partial(gradient, at), *refs_of_work)
                if at % span == span - 1:
                    for place in range(len(blocks)):
                        departure(place, piece).start()
            for piece in range(pieces):
                if send is None:
                    break
                part = slice(piece * width, (piece + 1) * width)
                for chunk in range(tokens // 128):
                    values = store[chunk, part.start * rows : part.stop * rows].astype(BF16)
                    lanes = slice(chunk * 128, (chunk + 1) * 128)
                    ready[part, :, lanes] = values.reshape(width, rows, 128)
                sending(piece).start()
            for piece in range(pieces):
                for place in range(len(blocks)):
                    departure(place, piece).wait()
                if send is not None:
                    sending(piece).wait()

        anywhere = pl.BlockSpec(memory_space=pl.ANY)
        here_already = [pl.BlockSpec(memory_space=pltpu.VMEM)] * direct
        volume = sum(math.prod(o.shape) * o.dtype.itemsize for o in operands + outs)
        products = (1 if matrices else 0) + (1 if grads else 0)
        flops = products * 2 * plan.own * plan.size * plan.size * tokens
        return pl.pallas_call(
            kernel,
            out_shape=outs,
            in_specs=[pl.BlockSpec(memory_space=pltpu.SMEM)]
            + here_already
            + [anywhere] * (len(operands) - direct),
            out_specs=[anywhere] * len(outs),
            scratch_shapes=scratch,
            input_output_aliases=aliases,
            compiler_params=pltpu.CompilerParams(vmem_limit_bytes=52 * 1024 * 1024),
            cost_estimate=pl.CostEstimate(flops=flops, bytes_accessed=volume, transcendentals=0),
            name=work.__name__,
        )(picks, *operands)


def two_segments(plan, inputs, factors, cotangent, sections):
    segment = lax.axis_index("segment")
    both = [(0, 1), (1, 0)]
    count = 3

    owners = [jnp.int32(0), 2 - sections[0], jnp.int32(1)]
    slots = [jnp.int32(0), sections[0] - 1, sections[1] - 1]
    picks = []
    for owner, slot in zip(owners, slots):
        picks += [jnp.clip(slot, 0, 1), (owner == segment).astype(jnp.int32)]
    kernels = Kernels(plan, inputs.shape[3], jnp.stack(picks).astype(jnp.int32))
    run = kernels.run

    def exchange(value):
        return lax.all_to_all(value, "blk", 0, 0, tiled=True)

    micro = lax.dynamic_index_in_dim(inputs, segment, 0, keepdims=False)
    grad = lax.dynamic_index_in_dim(cotangent, segment, 0, keepdims=False)
    early = [lax.ppermute(factor[0], "segment", [(0, 1)]) for factor in factors]

    first_has_two = sections[0] == 2
    middle, late = [], []
    for factor in factors:
        leave = jnp.where(segment == 0, factor[1], factor[0])
        middle.append(lax.ppermute(leave, "segment", both))
        last = lax.ppermute(factor[1], "segment", [(1, 0)])
        late.append(jnp.where(first_has_two, middle[-1], last))

    def weight(layer, at):
        return layer, factors[at], (early, middle, late)[layer][at]

    waiting = [(), ()]
    parts = [[None] * 4 for layer in range(count)]

    def step(layer, at, work, ins, packed=2, naturals=0, plain=False, **options):
        use = None if plain else weight(layer, at)
        after = waiting.pop(0) if waiting and not plain else ()
        results = run(work, ins, packed, use, naturals=naturals, grads=True, after=after, **options)
        *results, leave = results
        other = lax.ppermute(leave, "segment", [(1, 0)] if layer == 0 else both)
        if not plain:
            waiting.append((other,))
        parts[layer][at] = (leave, other)
        return results

    saved = []
    state = micro
    sent = run(start_work, (state,), 0, weight(0, 0))[0]
    inner = exchange(sent)
    upper = exchange(run(left_work, (inner,), 1, weight(0, 1))[0])
    inner_two = exchange(run(gelu_work, (upper,), 1, weight(0, 2))[0])
    branch = exchange(run(left_work, (inner_two,), 1, weight(0, 3))[0])
    saved.append((state, inner, upper, inner_two))

    beside = run(pack_work, (grad,), send=1)[0]
    ins = (branch, state)
    sent, state = run(residual_work, ins, 1, weight(1, 0), send=0, naturals=1, join=beside)
    values = exchange(sent)
    inner, last_grad_c = (values, 0), (values, 1)
    sent = run(left_work, (inner,), 1, weight(1, 1), after=(late[3],))[0]
    upper = exchange(sent)
    beside = run(last_back_left_work, (last_grad_c,), 1, weight(2, 3), send=1)[0]
    values = exchange(run(gelu_work, (upper,), 1, weight(1, 2), send=0, join=beside)[0])
    inner_two, last_grad_a = (values, 0), (values, 1)
    branch = exchange(run(left_work, (inner_two,), 1, weight(1, 3))[0])
    saved.append((state, inner, upper, inner_two))

    sent, state = run(residual_work, (branch, state), 1, weight(2, 0), naturals=1)
    inner = exchange(sent)
    upper = exchange(run(left_work, (inner,), 1, weight(2, 1))[0])

    sent = step(2, 2, back_gelu_work, (last_grad_a, upper))[0]
    beside = run(gelu_work, (upper,), 1, weight(2, 2), send=1)[0]
    sent = step(2, 1, back_left_work, (exchange(sent), inner), send=0, join=beside)[0]
    values = exchange(sent)
    grad_a, inner_two = (values, 0), (values, 1)
    sent, grad = step(2, 0, back_right_work, (grad_a, state, grad), 1, 1)
    step(2, 3, last_outer_work, (last_grad_c, inner_two), plain=True, send=None)
    for layer in (1, 0):
        state, inner, upper, inner_two = saved[layer]
        sent = step(layer, 3, back_left_work, (exchange(sent), inner_two))[0]
        sent = step(layer, 2, back_gelu_work, (exchange(sent), upper))[0]
        sent = step(layer, 1, back_left_work, (exchange(sent), inner))[0]
        if layer > 0:
            ins = (exchange(sent), state, grad)
            sent, grad = step(layer, 0, back_right_work, ins, 1, 1)
    step(0, 0, end_work, (exchange(sent), state), 1, plain=True, send=None)

    outs = []
    for at in range(4):
        zero, one, two = [
            stay.astype(F32) + other.astype(F32) for stay, other in (p[at] for p in parts)
        ]
        low = jnp.where(segment == 0, zero, jnp.where(first_has_two, two, one))
        high = jnp.where(segment == 0, one, two)
        high = jnp.where(first_has_two == (segment == 0), high, 0.0)
        outs.append(jnp.stack([low, high]))
    return tuple(outs)


def apply(weight, values):
    return jnp.einsum("bij,bit->bjt", weight, values, preferred_element_type=F32)


def apply_back(weight, values):
    return jnp.einsum("bij,bjt->bit", weight, values, preferred_element_type=F32)


def outer(values, grad):
    return jnp.einsum("bit,bjt->bij", values, grad, preferred_element_type=F32).astype(BF16)


def spread(plan, factor, owner, half):
    every = lax.all_gather(factor, "segment", axis=0)
    factor = lax.dynamic_index_in_dim(every, owner, 0, keepdims=False)
    if plan.halves == 1:
        return factor
    other = plan.swap_halves(factor)
    lower = jnp.where(half == 0, factor, other)
    upper = jnp.where(half == 0, other, factor)
    return jnp.concatenate([lower, upper], axis=1)


def collect(plan, parts, half):
    if plan.halves == 1:
        return lax.psum(parts.astype(F32), "segment")
    lower, upper = parts[:, : plan.own], parts[:, plan.own :]
    kept = jnp.where(half == 0, lower, upper)
    other = plan.swap_halves(jnp.where(half == 0, upper, lower))
    return lax.psum(kept.astype(F32) + other.astype(F32), "segment")


def token_chunk(plan, values, half):
    mine = lax.axis_index("segment")
    per_micro = values.shape[-1] // plan.tokens

    def chunk(at):
        at = mine * plan.halves + at
        micro = lax.dynamic_index_in_dim(values, at // per_micro, 0, keepdims=False)
        start = (at % per_micro) * plan.tokens
        return lax.dynamic_slice_in_dim(micro, start, plan.tokens, 2)

    if plan.halves == 1:
        return chunk(0)
    kept, other = chunk(half), plan.swap_halves(chunk(1 - half))
    lower = jnp.where(half == 0, kept, other)
    upper = jnp.where(half == 0, other, kept)
    return jnp.concatenate([lower, upper], axis=0)


def many_segments(plan, inputs, factors, cotangent, sections):
    segment = lax.axis_index("segment")
    half = lax.axis_index("blk") // plan.group
    slots = factors[0].shape[0]

    def trade(values):
        return plan.unpack(plan.exchange(plan.pack(values.astype(BF16))))

    count = plan.segments * slots - 1
    ends = jnp.cumsum(sections)
    layers, weights = [], []
    for index in range(count):
        owner = jnp.minimum(jnp.sum((index >= ends).astype(jnp.int32)), plan.segments - 1)
        slot = jnp.clip(index - (ends[owner] - sections[owner]), 0, slots - 1)
        layers.append((owner, slot, index < ends[-1]))
        picked = [lax.dynamic_index_in_dim(f, slot, 0, keepdims=True) for f in factors]
        weights.append(spread(plan, jnp.concatenate(picked, axis=0), owner, half))

    state = token_chunk(plan, inputs, half)
    grad = token_chunk(plan, cotangent, half)
    saved = []
    for index in range(count):
        w = weights[index]
        inner_one = trade(apply(w[0], state))
        upper = trade(apply(w[1], inner_one))
        hidden = gelu(upper.astype(F32)).astype(BF16)
        inner_two = trade(apply(w[2], hidden))
        saved.append((state, inner_one, upper, hidden, inner_two))
        if index < count - 1:
            branch = trade(apply(w[3], inner_two))
            total = (state.astype(F32) + branch.astype(F32)).astype(BF16)
            state = jnp.where(layers[index][2], total, state)

    totals = [None] * count
    for index in reversed(range(count)):
        w = weights[index]
        state, inner_one, upper, hidden, inner_two = saved[index]
        grad_c = trade(grad)
        grad_a = trade(apply_back(w[3], grad_c))
        parts = [outer(hidden, grad_a), outer(inner_two, grad_c)]
        grad_u = apply_back(w[2], grad_a) * gelu_slope(upper.astype(F32))
        grad_c = trade(grad_u)
        grad_a = trade(apply_back(w[1], grad_c))
        parts = [outer(state, grad_a), outer(inner_one, grad_c)] + parts
        totals[index] = collect(plan, jnp.stack(parts), half)
        total = (apply_back(w[0], grad_a) + grad.astype(F32)).astype(BF16)
        grad = jnp.where(layers[index][2], total, grad)

    outs = []
    for at in range(4):
        rows = []
        for place in range(slots):
            total = jnp.zeros(factors[0].shape[1:], F32)
            for index, (owner, slot, active) in enumerate(layers):
                here = active & (owner == segment) & (slot == place)
                total = jnp.where(here, totals[index][at], total)
            rows.append(total)
        outs.append(jnp.stack(rows))
    return tuple(outs)


def shards(inputs, first_right, first_left, second_right, second_left, cotangent, sections):
    segments = lax.axis_size("segment")
    devices = lax.axis_size("blk")
    plan = Plan(segments, devices, inputs.shape[0], inputs.shape[2], inputs.shape[3])
    factors = (first_right, first_left, second_right, second_left)
    run = two_segments if plan.kernels else many_segments
    return run(plan, inputs, factors, cotangent, sections)


def solution(mesh):
    whole = P("segment", "blk", None, None)
    tokens = P(None, "blk", None, None)
    in_specs = (tokens, whole, whole, whole, whole, tokens, P())
    return jax.shard_map(
        shards, mesh=mesh, in_specs=in_specs, out_specs=(whole,) * 4, check_vma=False
    )
```

```python
import functools
import math

import jax
import jax.numpy as jnp
from jax import lax
from jax.experimental import pallas as pl
from jax.experimental.pallas import tpu as pltpu
from jax.sharding import PartitionSpec as P

F32 = jnp.float32
BF16 = jnp.bfloat16
ROOT = math.sqrt(2.0 / math.pi)


def gelu(u):
    return 0.5 * u * (1.0 + jnp.tanh(ROOT * (u + 0.044715 * (u * u * u))))


def gelu_slope(u):
    square = u * u
    th = jnp.tanh(ROOT * (u + 0.044715 * (u * square)))
    inner = ROOT * (1.0 + 3 * 0.044715 * square)
    return 0.5 * (1.0 + th) + 0.5 * u * (1.0 - th * th) * inner


class Plan:
    def __init__(self, segments, devices, micros, blocks, tokens):
        self.segments = segments
        self.devices = devices
        self.halves = 2 if micros * tokens >= 256 * segments and devices % 2 == 0 else 1
        self.group = devices // self.halves
        self.own = blocks // devices
        self.held = self.own * self.halves
        self.size = blocks
        self.tokens = micros * tokens // (segments * self.halves)
        self.kernels = segments == 2 and micros == 2 and self.own == 8 and tokens % 128 == 0
        self.groups = None
        if self.halves > 1:
            self.groups = [
                [half * self.group + rank for rank in range(self.group)]
                for half in range(self.halves)
            ]

    def packed_shape(self):
        return (self.group, self.held, self.held, self.tokens)

    def natural_shape(self):
        return (self.held, self.size, self.tokens)

    def pack(self, values):
        split = values.reshape(self.held, self.halves, self.group, self.own, self.tokens)
        return split.transpose(2, 1, 3, 0, 4).reshape(self.packed_shape())

    def unpack(self, packed):
        split = packed.reshape(self.group, self.held, self.halves, self.own, self.tokens)
        return split.transpose(1, 2, 0, 3, 4).reshape(self.natural_shape())

    def exchange(self, packed):
        return lax.all_to_all(packed, "blk", 0, 0, axis_index_groups=self.groups, tiled=True)

    def swap_halves(self, value):
        return lax.ppermute(
            value, "blk", [(at, (at + self.group) % self.devices) for at in range(self.devices)]
        )


def matmul(a, b, over_a, over_b):
    return lax.dot_general(a, b, (((over_a,), (over_b,)), ((), ())), preferred_element_type=F32)


def read(plan, ref, at):
    pair = slice(at // 2 * 2 * plan.own, (at // 2 + 1) * 2 * plan.own)
    rows = ref[:, pair].astype(F32)[:, at % 2 * plan.own : (at % 2 + 1) * plan.own]
    return rows.reshape(plan.size, rows.shape[-1])


def start_work(plan, at, scatter, weight, gradient, state):
    scatter(matmul(weight, state[at], 0, 0))


def residual_work(plan, at, scatter, weight, gradient, branch, state, result):
    total = (state[at].astype(F32) + read(plan, branch, at)).astype(BF16)
    result[at] = total
    scatter(matmul(weight, total, 0, 0))


def left_work(plan, at, scatter, weight, gradient, values):
    scatter(matmul(weight, read(plan, values, at).astype(BF16), 0, 0))


def gelu_work(plan, at, scatter, weight, gradient, values):
    scatter(matmul(weight, gelu(read(plan, values, at)).astype(BF16), 0, 0))


def pack_work(plan, at, scatter, weight, gradient, values):
    scatter(values[at].astype(F32))


def last_back_left_work(plan, at, scatter, weight, gradient, grad):
    scatter(matmul(weight, read(plan, grad, at).astype(BF16), 1, 0))


def last_outer_work(plan, at, scatter, weight, gradient, grad, values):
    natural = read(plan, grad, at).astype(BF16)
    gradient(matmul(read(plan, values, at).astype(BF16), natural, 1, 1))


def back_left_work(plan, at, scatter, weight, gradient, grad, values):
    natural = read(plan, grad, at).astype(BF16)
    scatter(matmul(weight, natural, 1, 0))
    gradient(matmul(read(plan, values, at).astype(BF16), natural, 1, 1))


def back_gelu_work(plan, at, scatter, weight, gradient, grad, values):
    natural = read(plan, grad, at).astype(BF16)
    upper = read(plan, values, at)
    scatter(matmul(weight, natural, 1, 0) * gelu_slope(upper))
    gradient(matmul(gelu(upper).astype(BF16), natural, 1, 1))


def back_right_work(plan, at, scatter, weight, gradient, grad, state, above, result):
    natural = read(plan, grad, at).astype(BF16)
    total = matmul(weight, natural, 1, 0) + above[at].astype(F32)
    result[at] = total.astype(BF16)
    scatter(total)
    gradient(matmul(state[at], natural, 1, 1))


def end_work(plan, at, scatter, weight, gradient, grad, state):
    natural = read(plan, grad, at).astype(BF16)
    gradient(matmul(state[at], natural, 1, 1))


class Kernels:
    def __init__(self, plan, tokens, picks):
        self.plan = plan
        self.picks = picks
        self.tokens = tokens
        self.natural = (plan.own, plan.size, tokens)
        self.sent = (plan.devices, plan.own * plan.own, tokens)
        self.square = (plan.own, plan.size, plan.size)

    def run(
        self, work, ins, packed=0, weight=None, send=True, naturals=0, grads=False, after=(), join=None
    ):
        plan, tokens, picks = self.plan, self.tokens, self.picks
        rows = plan.own * plan.own
        pieces = 1
        span = plan.own // pieces
        arrays = [value[0] if isinstance(value, tuple) else value for value in ins]
        places = [value[1] if isinstance(value, tuple) else 0 for value in ins]
        direct = 1 if packed else 0
        layer, mine, theirs = weight or (0, None, None)
        matrices = [m for m in (mine, theirs) if m is not None]
        unread = list(after) + ([] if join is None else [join])
        operands = arrays + matrices + unread
        aliases = {} if join is None else {len(operands): 0}
        outs = []
        if send is not None:
            parts = 1 if send is True else 2
            outs.append(jax.ShapeDtypeStruct((plan.devices, parts * rows, tokens), BF16))
        outs += [jax.ShapeDtypeStruct(self.natural, BF16)] * naturals
        outs += [jax.ShapeDtypeStruct(self.square, BF16)] * (1 if grads else 0)
        blocks = outs[0 if send is None else 1 :]
        scratch = [pltpu.VMEM(self.sent, BF16)] * (packed - direct)
        scratch += [pltpu.VMEM(self.natural, BF16)] * (len(ins) - packed)
        scratch += [pltpu.VMEM(self.square, BF16)] * (1 if matrices else 0)
        scratch += [pltpu.VMEM(block.shape, block.dtype) for block in blocks]
        if send is not None:
            scratch.append(pltpu.VMEM(self.sent, BF16))
            scratch.append(pltpu.VMEM((tokens // 128, plan.size * plan.own, 128), F32))
        scratch.append(pltpu.SemaphoreType.DMA((len(ins) + 1, pieces)))
        scratch.append(pltpu.SemaphoreType.DMA((len(outs) + 1, pieces)))

        def kernel(picks, *refs):
            refs = list(refs)

            def take(count):
                return [refs.pop(0) for i in range(count)]

            sources, factors = take(len(ins)), take(len(matrices))
            take(len(unread))
            out = take(1)[0] if send is not None else None
            targets = take(len(blocks))
            inner = []
            if direct:
                inner.append(sources[0].at[:, pl.ds(places[0] * rows, rows)])
            inner += take(len(ins) - direct)
            matrix = take(1)[0] if matrices else None
            results = take(len(blocks))
            ready, store = take(2) if send is not None else (None, None)
            in_sems, out_sems = take(2)
            here = picks[2 * layer + 1] == 1

            def arrival(at, piece):
                source, target = sources[at], inner[at]
                if at < packed:
                    width = span * plan.own
                    source = source.at[:, pl.ds(places[at] * rows + piece * width, width)]
                    target = target.at[:, pl.ds(piece * width, width)]
                else:
                    source = source.at[pl.ds(piece * span, span)]
                    target = target.at[pl.ds(piece * span, span)]
                return pltpu.make_async_copy(source, target, in_sems.at[at, piece])

            def factor(which, piece):
                source = factors[which]
                if len(source.shape) == 4:
                    source = source.at[picks[2 * layer]]
                part = pl.ds(piece * span, span)
                sem = in_sems.at[len(ins), piece]
                return pltpu.make_async_copy(source.at[part], matrix.at[part], sem)

            def departure(at, piece):
                part = pl.ds(piece * span, span)
                sem = out_sems.at[at, piece]
                return pltpu.make_async_copy(results[at].at[part], targets[at].at[part], sem)

            width = plan.devices // pieces

            def sending(piece):
                part = pl.ds(piece * width, width)
                first = 0 if send is True else send * rows
                target = out.at[part, pl.ds(first, rows)]
                sem = out_sems.at[len(outs), piece]
                return pltpu.make_async_copy(ready.at[part], target, sem)

            for piece in range(pieces):
                if len(factors) == 2:

                    @pl.when(here)
                    def _():
                        factor(0, piece).start()

                    @pl.when(jnp.logical_not(here))
                    def _():
                        factor(1, piece).start()

                elif factors:
                    factor(0, piece).start()
                for at in range(direct, len(ins)):
                    arrival(at, piece).start()

            def scatter(at, values):
                spread = pl.ds(at, plan.size, stride=plan.own)
                for part in range(tokens // 128):
                    store[part, spread, :] = values[:, part * 128 : (part + 1) * 128]

            def gradient(at, values):
                for ref in results[naturals:]:
                    ref[at] = values.astype(ref.dtype)

            for at in range(plan.own):
                piece = at // span
                if at % span == 0:
                    if factors:
                        factor(0, piece).wait()
                    for place in range(direct, len(ins)):
                        arrival(place, piece).wait()
                put = functools.partial(scatter, at)
                used = matrix[at] if factors else None
                refs_of_work = inner + results[:naturals]
                work(plan, at, put, used, functools.partial(gradient, at), *refs_of_work)
                if at % span == span - 1:
                    for place in range(len(blocks)):
                        departure(place, piece).start()
            for piece in range(pieces):
                if send is None:
                    break
                part = slice(piece * width, (piece + 1) * width)
                for chunk in range(tokens // 128):
                    values = store[chunk, part.start * rows : part.stop * rows].astype(BF16)
                    lanes = slice(chunk * 128, (chunk + 1) * 128)
                    ready[part, :, lanes] = values.reshape(width, rows, 128)
                sending(piece).start()
            for piece in range(pieces):
                for place in range(len(blocks)):
                    departure(place, piece).wait()
                if send is not None:
                    sending(piece).wait()

        anywhere = pl.BlockSpec(memory_space=pl.ANY)
        here_already = [pl.BlockSpec(memory_space=pltpu.VMEM)] * direct
        volume = sum(math.prod(o.shape) * o.dtype.itemsize for o in operands + outs)
        products = (1 if matrices else 0) + (1 if grads else 0)
        flops = products * 2 * plan.own * plan.size * plan.size * tokens
        return pl.pallas_call(
            kernel,
            out_shape=outs,
            in_specs=[pl.BlockSpec(memory_space=pltpu.SMEM)]
            + here_already
            + [anywhere] * (len(operands) - direct),
            out_specs=[anywhere] * len(outs),
            scratch_shapes=scratch,
            input_output_aliases=aliases,
            compiler_params=pltpu.CompilerParams(vmem_limit_bytes=52 * 1024 * 1024),
            cost_estimate=pl.CostEstimate(flops=flops, bytes_accessed=volume, transcendentals=0),
            name=work.__name__,
        )(picks, *operands)


def two_segments(plan, inputs, factors, cotangent, sections):
    segment = lax.axis_index("segment")
    both = [(0, 1), (1, 0)]
    count = 3

    owners = [jnp.int32(0), 2 - sections[0], jnp.int32(1)]
    slots = [jnp.int32(0), sections[0] - 1, sections[1] - 1]
    picks = []
    for owner, slot in zip(owners, slots):
        picks += [jnp.clip(slot, 0, 1), (owner == segment).astype(jnp.int32)]
    kernels = Kernels(plan, inputs.shape[3], jnp.stack(picks).astype(jnp.int32))
    run = kernels.run

    def exchange(value):
        return lax.all_to_all(value, "blk", 0, 0, tiled=True)

    micro = lax.dynamic_index_in_dim(inputs, segment, 0, keepdims=False)
    grad = lax.dynamic_index_in_dim(cotangent, segment, 0, keepdims=False)
    early = [lax.ppermute(factor[0], "segment", [(0, 1)]) for factor in factors]

    first_has_two = sections[0] == 2
    middle, late = [], []
    for factor in factors:
        leave = jnp.where(segment == 0, factor[1], factor[0])
        middle.append(lax.ppermute(leave, "segment", both))
        last = lax.ppermute(factor[1], "segment", [(1, 0)])
        late.append(jnp.where(first_has_two, middle[-1], last))

    def weight(layer, at):
        return layer, factors[at], (early, middle, late)[layer][at]

    waiting = [(), ()]
    parts = [[None] * 4 for layer in range(count)]

    def step(layer, at, work, ins, packed=2, naturals=0, plain=False, **options):
        use = None if plain else weight(layer, at)
        after = waiting.pop(0) if waiting and not plain else ()
        results = run(work, ins, packed, use, naturals=naturals, grads=True, after=after, **options)
        *results, leave = results
        other = lax.ppermute(leave, "segment", [(1, 0)] if layer == 0 else both)
        if not plain:
            waiting.append((other,))
        parts[layer][at] = (leave, other)
        return results

    saved = []
    state = micro
    sent = run(start_work, (state,), 0, weight(0, 0))[0]
    inner = exchange(sent)
    upper = exchange(run(left_work, (inner,), 1, weight(0, 1))[0])
    inner_two = exchange(run(gelu_work, (upper,), 1, weight(0, 2))[0])
    branch = exchange(run(left_work, (inner_two,), 1, weight(0, 3))[0])
    saved.append((state, inner, upper, inner_two))

    beside = run(pack_work, (grad,), send=1)[0]
    ins = (branch, state)
    sent, state = run(residual_work, ins, 1, weight(1, 0), send=0, naturals=1, join=beside)
    values = exchange(sent)
    inner, last_grad_c = (values, 0), (values, 1)
    sent = run(left_work, (inner,), 1, weight(1, 1), after=(late[3],))[0]
    upper = exchange(sent)
    beside = run(last_back_left_work, (last_grad_c,), 1, weight(2, 3), send=1)[0]
    values = exchange(run(gelu_work, (upper,), 1, weight(1, 2), send=0, join=beside)[0])
    inner_two, last_grad_a = (values, 0), (values, 1)
    branch = exchange(run(left_work, (inner_two,), 1, weight(1, 3))[0])
    saved.append((state, inner, upper, inner_two))

    sent, state = run(residual_work, (branch, state), 1, weight(2, 0), naturals=1)
    inner = exchange(sent)
    upper = exchange(run(left_work, (inner,), 1, weight(2, 1))[0])

    sent = step(2, 2, back_gelu_work, (last_grad_a, upper))[0]
    beside = run(gelu_work, (upper,), 1, weight(2, 2), send=1)[0]
    sent = step(2, 1, back_left_work, (exchange(sent), inner), send=0, join=beside)[0]
    values = exchange(sent)
    grad_a, inner_two = (values, 0), (values, 1)
    sent, grad = step(2, 0, back_right_work, (grad_a, state, grad), 1, 1)
    step(2, 3, last_outer_work, (last_grad_c, inner_two), plain=True, send=None)
    for layer in (1, 0):
        state, inner, upper, inner_two = saved[layer]
        sent = step(layer, 3, back_left_work, (exchange(sent), inner_two))[0]
        sent = step(layer, 2, back_gelu_work, (exchange(sent), upper))[0]
        sent = step(layer, 1, back_left_work, (exchange(sent), inner))[0]
        if layer > 0:
            ins = (exchange(sent), state, grad)
            sent, grad = step(layer, 0, back_right_work, ins, 1, 1)
    step(0, 0, end_work, (exchange(sent), state), 1, plain=True, send=None)

    outs = []
    for at in range(4):
        zero, one, two = [
            stay.astype(F32) + other.astype(F32) for stay, other in (p[at] for p in parts)
        ]
        low = jnp.where(segment == 0, zero, jnp.where(first_has_two, two, one))
        high = jnp.where(segment == 0, one, two)
        high = jnp.where(first_has_two == (segment == 0), high, 0.0)
        outs.append(jnp.stack([low, high]))
    return tuple(outs)


def apply(weight, values):
    return jnp.einsum("bij,bit->bjt", weight, values, preferred_element_type=F32)


def apply_back(weight, values):
    return jnp.einsum("bij,bjt->bit", weight, values, preferred_element_type=F32)


def outer(values, grad):
    return jnp.einsum("bit,bjt->bij", values, grad, preferred_element_type=F32).astype(BF16)


def spread(plan, factor, owner, half):
    every = lax.all_gather(factor, "segment", axis=0)
    factor = lax.dynamic_index_in_dim(every, owner, 0, keepdims=False)
    if plan.halves == 1:
        return factor
    other = plan.swap_halves(factor)
    lower = jnp.where(half == 0, factor, other)
    upper = jnp.where(half == 0, other, factor)
    return jnp.concatenate([lower, upper], axis=1)


def collect(plan, parts, half):
    if plan.halves == 1:
        return lax.psum(parts.astype(F32), "segment")
    lower, upper = parts[:, : plan.own], parts[:, plan.own :]
    kept = jnp.where(half == 0, lower, upper)
    other = plan.swap_halves(jnp.where(half == 0, upper, lower))
    return lax.psum(kept.astype(F32) + other.astype(F32), "segment")


def token_chunk(plan, values, half):
    mine = lax.axis_index("segment")
    per_micro = values.shape[-1] // plan.tokens

    def chunk(at):
        at = mine * plan.halves + at
        micro = lax.dynamic_index_in_dim(values, at // per_micro, 0, keepdims=False)
        start = (at % per_micro) * plan.tokens
        return lax.dynamic_slice_in_dim(micro, start, plan.tokens, 2)

    if plan.halves == 1:
        return chunk(0)
    kept, other = chunk(half), plan.swap_halves(chunk(1 - half))
    lower = jnp.where(half == 0, kept, other)
    upper = jnp.where(half == 0, other, kept)
    return jnp.concatenate([lower, upper], axis=0)


def many_segments(plan, inputs, factors, cotangent, sections):
    segment = lax.axis_index("segment")
    half = lax.axis_index("blk") // plan.group
    slots = factors[0].shape[0]

    def trade(values):
        return plan.unpack(plan.exchange(plan.pack(values.astype(BF16))))

    count = plan.segments * slots - 1
    ends = jnp.cumsum(sections)
    layers, weights = [], []
    for index in range(count):
        owner = jnp.minimum(jnp.sum((index >= ends).astype(jnp.int32)), plan.segments - 1)
        slot = jnp.clip(index - (ends[owner] - sections[owner]), 0, slots - 1)
        layers.append((owner, slot, index < ends[-1]))
        picked = [lax.dynamic_index_in_dim(f, slot, 0, keepdims=True) for f in factors]
        weights.append(spread(plan, jnp.concatenate(picked, axis=0), owner, half))

    state = token_chunk(plan, inputs, half)
    grad = token_chunk(plan, cotangent, half)
    saved = []
    for index in range(count):
        w = weights[index]
        inner_one = trade(apply(w[0], state))
        upper = trade(apply(w[1], inner_one))
        hidden = gelu(upper.astype(F32)).astype(BF16)
        inner_two = trade(apply(w[2], hidden))
        saved.append((state, inner_one, upper, hidden, inner_two))
        if index < count - 1:
            branch = trade(apply(w[3], inner_two))
            total = (state.astype(F32) + branch.astype(F32)).astype(BF16)
            state = jnp.where(layers[index][2], total, state)

    totals = [None] * count
    for index in reversed(range(count)):
        w = weights[index]
        state, inner_one, upper, hidden, inner_two = saved[index]
        grad_c = trade(grad)
        grad_a = trade(apply_back(w[3], grad_c))
        parts = [outer(hidden, grad_a), outer(inner_two, grad_c)]
        grad_u = apply_back(w[2], grad_a) * gelu_slope(upper.astype(F32))
        grad_c = trade(grad_u)
        grad_a = trade(apply_back(w[1], grad_c))
        parts = [outer(state, grad_a), outer(inner_one, grad_c)] + parts
        totals[index] = collect(plan, jnp.stack(parts), half)
        total = (apply_back(w[0], grad_a) + grad.astype(F32)).astype(BF16)
        grad = jnp.where(layers[index][2], total, grad)

    outs = []
    for at in range(4):
        rows = []
        for place in range(slots):
            total = jnp.zeros(factors[0].shape[1:], F32)
            for index, (owner, slot, active) in enumerate(layers):
                here = active & (owner == segment) & (slot == place)
                total = jnp.where(here, totals[index][at], total)
            rows.append(total)
        outs.append(jnp.stack(rows))
    return tuple(outs)


def shards(inputs, first_right, first_left, second_right, second_left, cotangent, sections):
    segments = lax.axis_size("segment")
    devices = lax.axis_size("blk")
    plan = Plan(segments, devices, inputs.shape[0], inputs.shape[2], inputs.shape[3])
    factors = (first_right, first_left, second_right, second_left)
    run = two_segments if plan.kernels else many_segments
    return run(plan, inputs, factors, cotangent, sections)


def solution(mesh):
    whole = P("segment", "blk", None, None)
    tokens = P(None, "blk", None, None)
    in_specs = (tokens, whole, whole, whole, whole, tokens, P())
    return jax.shard_map(
        shards, mesh=mesh, in_specs=in_specs, out_specs=(whole,) * 4, check_vma=False
    )
```
